256 devices in a mesh: gx: 128 (over z, x, y), gy: 2 (over core).
Axes of the slice: x: 4, y: 4, z: 8, core: 2. Of those that a mesh axis runs over, the one named last changes fastest.
Arguments:
- log_perm: float32 [4, 128, 256, 256], P(None, 'gx', None, 'gy'), may hold values from -4 to 4
- recharge: float32 [4, 256, 256], P(None, None, 'gy'), may hold values from -24 to 24
- well_cells: int32 [32], replicated, may hold values from 0 to 262143
- observed: float32 [32], replicated, may hold values from -5 to 5
- variances: float32 [32], replicated, may hold values from 0.02 to 0.2
- well_order: int32 [8], replicated, may hold values from 0 to 31
Outputs:
- post_perm: float32 [4, 128, 256, 256], P(None, None, 'gx', 'gy')
- post_head: float32 [4, 128, 256, 256], P(None, None, 'gx', 'gy')
The draws below stay inside these ranges and needn't reach their ends.
Inputs may be any that keep to these rules, and one draw needn't show every extreme that they name: `well_cells`: each entry is a flat cell index layer * 256 * 256 + row * 256 + column; wells may share a cell. `well_order`: wells may repeat or be absent.
All inputs are finite; a program needn't handle non-finite values.
Results may differ from the reference program's by a relative error of at most 0.0003.
Values sent between devices are 32-bit elements; how exact they have to be, the bound alone decides.
No kernel may reach another device: no remote copies, remote signals or barrier semaphores. Data moves between devices by JAX's collectives and lax.ppermute only.
A program may use at most 64 MiB of HBM per device.

```python
import math
import jax
import jax.numpy as jnp
from jax import lax

LAYERS = 4
PASSES = 8
WELLS = 32
STEPS = 8
MEMBERS = 128
NX = 256
NY = 256


def touch_ends(result, stream_key, low, largest):
    longest = result.shape.index(max(result.shape))
    spots = []
    for shift in (0, 1):
        where = [jax.random.randint(jax.random.fold_in(stream_key, axis), (), 0, length) for axis, length in enumerate(result.shape)]
        where[longest] = (where[longest] + shift) % result.shape[longest]
        spots.append(tuple(where))
    return result.at[spots[0]].set(low).at[spots[1]].set(largest)


def shard_levels(stream_key, shape, shards, smallest, top_value):
    loudness = 1.0
    for position, parts in shards:
        heights = jax.random.uniform(jax.random.fold_in(jax.random.fold_in(stream_key, 6), position), (parts,), jnp.float32, smallest / len(shards), top_value / len(shards))
        loudness = loudness * jnp.repeat(jnp.exp(heights), shape[position] // parts).reshape((-1,) + (1,) * (len(shape) - 1 - position))
    return loudness


def bell_draw(key, dims, scale, reach, cuts=(), held_as=jnp.bfloat16):
    values = jax.random.normal(key, dims, jnp.float32) * scale
    if len(cuts) > 0:
        values = shard_levels(key, dims, cuts, -0.22, 0.18) * values
    return jnp.clip(values, min=-reach, max=reach).astype(held_as)


def setup_inputs(seed: int = 0) -> dict:
    keys = jax.random.split(jax.random.key(seed), 7)
    log_perm = bell_draw(keys[0], (LAYERS, MEMBERS, NX, NY), 1.0, 4.0, ((1, 128), (3, 2)), jnp.float32)
    recharge = bell_draw(keys[1], (LAYERS, NX, NY), 4.0, 24.0, ((2, 2),), jnp.float32)
    well_cells = touch_ends(jax.random.randint(keys[2], (WELLS,), 0, LAYERS * NX * NY), jax.random.fold_in(keys[2], 1), 0, (LAYERS * NX * NY) - 1).astype(jnp.int32)
    observed = bell_draw(keys[3], (WELLS,), 1.0, 5.0, (), jnp.float32)
    variances = jnp.clip(jnp.exp(jax.random.uniform(keys[4], (WELLS,), jnp.float32, math.log(0.02), math.log(0.2))), 0.02, 0.2)
    well_order = touch_ends(jax.random.randint(keys[5], (STEPS,), 0, WELLS), jax.random.fold_in(keys[5], 1), 0, WELLS - 1).astype(jnp.int32)
    return {"log_perm": log_perm, "recharge": recharge, "well_cells": well_cells, "observed": observed, "variances": variances, "well_order": well_order}


VERT = 0.1
LEAK = 0.1

def harmonic(first, second):
    return 2.0 * first * second / (first + second)

def pad_sides(field):
    return jnp.pad(field, ((0, 0), (0, 0), (1, 1), (1, 1)))

def coefficients(centre, padded):
    north = harmonic(centre, padded[:, :, :-2, 1:-1])
    south = harmonic(centre, padded[:, :, 2:, 1:-1])
    west = harmonic(centre, padded[:, :, 1:-1, :-2])
    east = harmonic(centre, padded[:, :, 1:-1, 2:])
    vertical = VERT * harmonic(centre[1:], centre[:-1])
    zero_layer = jnp.zeros_like(centre[:1])
    upper = jnp.concatenate([zero_layer, vertical], 0)
    lower = jnp.concatenate([vertical, zero_layer], 0)
    diagonal = LEAK + north + south + west + east + upper + lower
    return (north, south, west, east, upper, lower, diagonal)

def relax(head_pad, head, coef, source):
    north, south, west, east, upper, lower, diagonal = coef
    zero_layer = jnp.zeros_like(head[:1])
    total = north * head_pad[:, :, :-2, 1:-1] + south * head_pad[:, :, 2:, 1:-1]
    total = total + west * head_pad[:, :, 1:-1, :-2] + east * head_pad[:, :, 1:-1, 2:]
    total = total + upper * jnp.concatenate([zero_layer, head[:-1]], 0)
    total = total + lower * jnp.concatenate([head[1:], zero_layer], 0)
    return (source + total) / diagonal

def well_terms(row, obs_value, variance):
    members = row.shape[0]
    mean_value = jnp.mean(row)
    spread = row - mean_value
    denom = jnp.sum(spread * spread) / (members - 1) + variance
    alpha = 1.0 / (1.0 + jnp.sqrt(variance / denom))
    weights = obs_value - mean_value - alpha * spread
    factor = 1.0 / ((members - 1) * denom)
    return (spread, factor, weights)

def assimilate_field(field, spread, factor, weights):
    covar = jnp.einsum('lmrc,m->lrc', field, spread, precision=lax.Precision.HIGHEST)
    return field + (covar * factor)[:, None] * weights[None, :, None, None]

def reference(log_perm, recharge, well_cells, observed, variances, well_order):
    centre = jnp.exp(log_perm)
    coef = coefficients(centre, jnp.exp(pad_sides(log_perm)))
    source = recharge[:, None]
    head = jnp.zeros_like(log_perm)
    for sweep in range(PASSES):
        head = relax(pad_sides(head), head, coef, source)

    def step(k, carry):
        perm_state, head_state = carry
        well = well_order[k]
        index = well_cells[well]
        layer = (index // (NX * NY)).astype(jnp.int32)
        row = (index // NY % NX).astype(jnp.int32)
        column = (index % NY).astype(jnp.int32)
        zero_index = jnp.int32(0)
        values = lax.dynamic_slice(head_state, (layer, zero_index, row, column), (1, MEMBERS, 1, 1)).reshape(MEMBERS)
        spread, factor, weights = well_terms(values, observed[well], variances[well])
        perm_state = assimilate_field(perm_state, spread, factor, weights)
        head_state = assimilate_field(head_state, spread, factor, weights)
        return (perm_state, head_state)
    post_perm, post_head = lax.fori_loop(0, STEPS, step, (log_perm, head))
    return (post_perm, post_head)
```

```python
import functools

import jax
import jax.numpy as jnp
from jax import lax
from jax.experimental import pallas as pl
from jax.experimental.pallas import tpu as pltpu
from jax.sharding import PartitionSpec as P

PASSES = 8
STEPS = 8
VERT = 0.1
LEAK = 0.1
HALO = 8
PAD = 8
CHUNK = 32
HIGHEST = lax.Precision.HIGHEST

VMEM = pl.BlockSpec(memory_space=pltpu.VMEM)
SMEM = pl.BlockSpec(memory_space=pltpu.SMEM)
PARAMS = pltpu.CompilerParams(vmem_limit_bytes=48 * 1024 * 1024)


def edges_kernel(core_ref, perm_ref, rech_ref, near_ref, away_ref):
    layers, rows, columns = perm_ref.shape
    core = core_ref[0]
    lane = lax.broadcasted_iota(jnp.int32, (2 * HALO, columns), 1)
    slot = lax.broadcasted_iota(jnp.int32, (2 * HALO, columns), 0)
    depth = jnp.where(slot < HALO, slot, 2 * HALO - 1 - slot)
    wanted = jnp.where(core == 0, columns - 1 - depth, depth)
    pick = (lane == wanted).astype(jnp.float32)
    for which, ref in enumerate((perm_ref, rech_ref)):
        for layer in range(layers):
            both = lax.dot_general(
                pick, ref[layer], (((1,), (1,)), ((), ())), precision=HIGHEST,
                preferred_element_type=jnp.float32,
            )
            near_ref[which, layer] = both[:HALO]
            away_ref[which, layer] = both[HALO:]


def pack_rows(load, send_ref, layers, rows, stride):
    for layer in range(layers):
        for r in range(2):
            for g in range(0, rows // 2, 8):
                send_ref[pl.ds(stride * g + 2 * layer + r, 8, stride=stride), :] = load(layer, 2 * g + r)


def pack_kernel(perm_ref, send_ref):
    layers, rows, _ = perm_ref.shape
    pack_rows(
        lambda layer, start: perm_ref[layer, pl.ds(start, 8, stride=2), :],
        send_ref, layers, rows, 2 * layers,
    )


def harmonic_inv(a, b):
    return 2.0 / (a + b)


def strip_heads(near_ref, far_ref):
    layers = near_ref.shape[1]
    rows = near_ref.shape[3]
    lane = lax.broadcasted_iota(jnp.int32, (2 * HALO, rows), 1)
    first, last = lane == 0, lane == rows - 1
    inv, source = [], []
    for layer in range(layers):
        inv.append(jnp.exp(-jnp.concatenate([far_ref[0, layer], near_ref[0, layer]], 0)))
        source.append(jnp.concatenate([far_ref[1, layer], near_ref[1, layer]], 0))
    vertical = [VERT * harmonic_inv(inv[i], inv[i + 1]) for i in range(layers - 1)]
    coef = []
    for layer in range(layers):
        a = inv[layer]
        north = harmonic_inv(a, jnp.where(first, 1.0, pltpu.roll(a, 1, 1)))
        south = harmonic_inv(a, jnp.where(last, 1.0, pltpu.roll(a, rows - 1, 1)))
        west = harmonic_inv(a, pltpu.roll(a, 1, 0))
        east = harmonic_inv(a, pltpu.roll(a, 2 * HALO - 1, 0))
        diag = LEAK + north + south + west + east
        if layer > 0:
            diag = diag + vertical[layer - 1]
        if layer < layers - 1:
            diag = diag + vertical[layer]
        scale = 1.0 / diag
        terms = [
            jnp.where(first, 0.0, north * scale), jnp.where(last, 0.0, south * scale),
            west * scale, east * scale,
            vertical[layer - 1] * scale if layer > 0 else None,
            vertical[layer] * scale if layer < layers - 1 else None,
            source[layer] * scale,
        ]
        coef.append(terms)
    head = [coef[layer][6] for layer in range(layers)]
    kept = [head[layer][HALO - 1:HALO] for layer in range(layers)]
    for _ in range(PASSES - 2):
        fresh = []
        for layer in range(layers):
            north, south, west, east, upper, lower, base = coef[layer]
            h = head[layer]
            total = base + north * pltpu.roll(h, 1, 1) + south * pltpu.roll(h, rows - 1, 1)
            total = total + west * pltpu.roll(h, 1, 0) + east * pltpu.roll(h, 2 * HALO - 1, 0)
            if upper is not None:
                total = total + upper * head[layer - 1]
            if lower is not None:
                total = total + lower * head[layer + 1]
            fresh.append(total)
        head = fresh
        kept += [head[layer][HALO - 1:HALO] for layer in range(layers)]
    kept += [inv[layer][HALO - 1:HALO] for layer in range(layers)]
    return jnp.concatenate(kept, 0)


def jacobi_kernel(
    core_ref, cells_ref, order_ref, perm_ref, rech_ref, near_ref, far_ref,
    send_ref,
    inv, rowt, vert, cn, cs, cw, ce, cu, cd, base, head_a, head_b, halo,
):
    layers, rows, columns = perm_ref.shape
    core = core_ref[0]
    stripe = lax.broadcasted_iota(jnp.int32, (CHUNK, columns), 1)
    west_cut = jnp.logical_and(stripe == 0, core == 1)
    east_cut = jnp.logical_and(stripe == columns - 1, core == 0)
    west_end = jnp.logical_and(stripe == 0, core == 0)
    east_end = jnp.logical_and(stripe == columns - 1, core == 1)
    edge_lane = jnp.where(core == 0, columns - 1, 0)

    kept = strip_heads(near_ref, far_ref)
    count = kept.shape[0]
    halo[...] = jnp.concatenate([kept, jnp.zeros((columns - count, rows), jnp.float32)], 0).T

    def shift_of(index):
        return lax.rem(edge_lane - index + columns, columns)

    ones = jnp.ones((PAD, columns), jnp.float32)
    zeros = jnp.zeros((PAD, columns), jnp.float32)
    for layer in range(layers):
        inv[layer, 0:PAD, :] = ones
        inv[layer, PAD + rows:2 * PAD + rows, :] = ones
        for ref in (head_a, head_b):
            ref[layer, 0:PAD, :] = zeros
            ref[layer, PAD + rows:2 * PAD + rows, :] = zeros
        for r in range(0, rows, CHUNK):
            inv[layer, PAD + r:PAD + r + CHUNK, :] = jnp.exp(-perm_ref[layer, r:r + CHUNK, :])
    for layer in range(layers):
        rowt[layer, 0:PAD, :] = harmonic_inv(inv[layer, 0:PAD, :], inv[layer, 1:PAD + 1, :])
        for r in range(0, rows, CHUNK):
            here = inv[layer, PAD + r:PAD + r + CHUNK, :]
            rowt[layer, PAD + r:PAD + r + CHUNK, :] = harmonic_inv(
                here, inv[layer, PAD + r + 1:PAD + r + CHUNK + 1, :]
            )
            if layer < layers - 1:
                vert[layer, r:r + CHUNK, :] = VERT * harmonic_inv(
                    here, inv[layer + 1, PAD + r:PAD + r + CHUNK, :]
                )
    for layer in range(layers):
        shift = shift_of(count - layers + layer)
        for r in range(0, rows, CHUNK):
            part = pl.ds(r, CHUNK)
            here = inv[layer, PAD + r:PAD + r + CHUNK, :]
            beyond = pltpu.roll(halo[part, :], shift, 1)
            inv_w = jnp.where(west_cut, beyond, jnp.where(west_end, 1.0, pltpu.roll(here, 1, 1)))
            inv_e = jnp.where(east_cut, beyond, jnp.where(east_end, 1.0, pltpu.roll(here, columns - 1, 1)))
            west = harmonic_inv(here, inv_w)
            east = harmonic_inv(here, inv_e)
            north = rowt[layer, PAD + r - 1:PAD + r + CHUNK - 1, :]
            south = rowt[layer, PAD + r:PAD + r + CHUNK, :]
            diag = LEAK + north + south + west + east
            if layer > 0:
                diag = diag + vert[layer - 1, part, :]
            if layer < layers - 1:
                diag = diag + vert[layer, part, :]
            scale = 1.0 / diag
            cn[layer, part, :] = north * scale
            cs[layer, part, :] = south * scale
            cw[layer, part, :] = jnp.where(west_end, 0.0, west * scale)
            ce[layer, part, :] = jnp.where(east_end, 0.0, east * scale)
            if layer > 0:
                cu[layer, part, :] = vert[layer - 1, part, :] * scale
            if layer < layers - 1:
                cd[layer, part, :] = vert[layer, part, :] * scale
            first = rech_ref[layer, part, :] * scale
            base[layer, part, :] = first
            head_a[layer, PAD + r:PAD + r + CHUNK, :] = first

    old, new = head_a, head_b
    for sweep in range(PASSES - 1):
        for layer in range(layers):
            shift = shift_of(sweep * layers + layer)
            for r in range(0, rows, CHUNK):
                part = pl.ds(r, CHUNK)
                h = old[layer, PAD + r:PAD + r + CHUNK, :]
                beyond = pltpu.roll(halo[part, :], shift, 1)
                total = base[layer, part, :]
                total = total + cn[layer, part, :] * old[layer, PAD + r - 1:PAD + r + CHUNK - 1, :]
                total = total + cs[layer, part, :] * old[layer, PAD + r + 1:PAD + r + CHUNK + 1, :]
                total = total + cw[layer, part, :] * jnp.where(west_cut, beyond, pltpu.roll(h, 1, 1))
                total = total + ce[layer, part, :] * jnp.where(east_cut, beyond, pltpu.roll(h, columns - 1, 1))
                if layer > 0:
                    total = total + cu[layer, part, :] * old[layer - 1, PAD + r:PAD + r + CHUNK, :]
                if layer < layers - 1:
                    total = total + cd[layer, part, :] * old[layer + 1, PAD + r:PAD + r + CHUNK, :]
                new[layer, PAD + r:PAD + r + CHUNK, :] = total
        old, new = new, old

    stride = 2 * layers + 1
    pack_rows(
        lambda layer, start: old[layer, pl.ds(PAD + start, 8, stride=2), :],
        send_ref, layers, rows, stride,
    )
    lane = lax.broadcasted_iota(jnp.int32, (1, columns), 1)
    wells = jnp.zeros((1, columns), jnp.float32)
    for k in range(STEPS):
        cell = cells_ref[order_ref[k]]
        width = 2 * columns
        layer = cell // (rows * width)
        row = cell // width % rows
        column = cell % width
        line = old[layer, pl.ds(PAD + row, 1), :]
        moved = pltpu.roll(line, lax.rem(k - column % columns + columns, columns), 1)
        mine = jnp.logical_and(lane == k, column // columns == core)
        wells = wells + jnp.where(mine, moved, 0.0)
    block = jnp.broadcast_to(wells, (8, columns))
    for g in range(0, rows // 2, 8):
        send_ref[pl.ds(stride * g + stride - 1, 8, stride=stride), :] = block


def wells_kernel(recv_ref, wells_ref):
    members = 128
    stride = recv_ref.shape[0] // members
    wells_ref[...] = recv_ref[pl.ds(stride - 1, members, stride=stride), :].T[:STEPS]


def apply_map(recv_ref, mix, out_ref, stride):
    members = mix.shape[0]
    for layer in range(4):
        for r in range(2):
            x = recv_ref[pl.ds(2 * layer + r, members, stride=stride), :]
            out_ref[pl.ds(layer * 2 * members + r, members, stride=2), :] = x + lax.dot_general(
                mix, x, (((1,), (0,)), ((), ())), precision=HIGHEST, preferred_element_type=jnp.float32
            )


def update_kernel(order_ref, obs_ref, var_ref, recv_ref, own_ref, other_ref, out_ref, mix_ref):
    members = own_ref.shape[1]
    y = own_ref[...] + other_ref[...]
    step_id = lax.broadcasted_iota(jnp.int32, y.shape, 0)
    gains = jnp.zeros_like(y)
    weights_all = jnp.zeros_like(y)
    for k in range(STEPS):
        well = order_ref[k]
        row = y[k:k + 1]
        mean_value = jnp.sum(row, axis=1, keepdims=True) * (1.0 / members)
        spread = row - mean_value
        variance = jnp.full((1, 1), var_ref[well], jnp.float32)
        denom = jnp.sum(spread * spread, axis=1, keepdims=True) / (members - 1) + variance
        alpha = 1.0 / (1.0 + jnp.sqrt(variance / denom))
        weights = (obs_ref[well] - mean_value) - alpha * spread
        factor = 1.0 / ((members - 1) * denom)
        earlier = jnp.sum(weights_all * spread, axis=1, keepdims=True)
        gain = factor * (spread + jnp.sum(gains * earlier, axis=0, keepdims=True))
        y = y + (factor * jnp.sum(y * spread, axis=1, keepdims=True)) * weights
        gains = jnp.where(step_id == k, gain, gains)
        weights_all = jnp.where(step_id == k, weights, weights_all)
    mix = lax.dot_general(
        weights_all, gains, (((0,), (0,)), ((), ())), precision=HIGHEST,
        preferred_element_type=jnp.float32,
    )
    mix_ref[...] = mix
    apply_map(recv_ref, mix, out_ref, recv_ref.shape[0] // members)


def perm_kernel(recv_ref, mix_ref, out_ref):
    apply_map(recv_ref, mix_ref[...], out_ref, recv_ref.shape[0] // mix_ref.shape[0])


def call(kernel, out, in_specs, scratch=()):
    return pl.pallas_call(
        kernel, out_shape=out, in_specs=in_specs,
        out_specs=jax.tree.map(lambda _: VMEM, out),
        scratch_shapes=list(scratch), compiler_params=PARAMS,
    )


def f32(*shape):
    return jax.ShapeDtypeStruct(shape, jnp.float32)


def exchange(send, parts):
    rows = send.shape[0] // parts
    moved = lax.all_to_all(
        send.reshape(parts, rows, 1, send.shape[1]), "gx", split_axis=0, concat_axis=0, tiled=True
    )
    return moved.reshape(send.shape)


def body(log_perm, recharge, well_cells, observed, variances, well_order):
    layers, _, rows, columns = log_perm.shape
    parts = lax.axis_size("gx")
    core = lax.axis_index("gy").astype(jnp.int32).reshape(1)
    swap = [(0, 1), (1, 0)]
    perm = log_perm.reshape(layers, rows, columns)
    near, away = call(
        edges_kernel, (f32(2, layers, HALO, rows),) * 2, [SMEM, VMEM, VMEM]
    )(core, perm, recharge)
    far = lax.ppermute(away, "gy", swap)
    perm_send = call(pack_kernel, f32(parts * 8, columns), [VMEM])(perm)
    field = pltpu.VMEM((layers, rows, columns), jnp.float32)
    padded = pltpu.VMEM((layers, rows + 2 * PAD, columns), jnp.float32)
    head_send = call(
        jacobi_kernel, f32(parts * 9, columns), [SMEM] * 3 + [VMEM] * 4,
        [padded, padded] + [field] * 8 + [padded, padded, pltpu.VMEM((rows, columns), jnp.float32)],
    )(core, well_cells, well_order, perm, recharge, near, far)
    head_send, perm_send = lax.optimization_barrier((head_send, perm_send))
    head_recv = exchange(head_send, parts)
    perm_recv = exchange(perm_send, parts)
    own = call(wells_kernel, f32(STEPS, parts), [VMEM])(head_recv)
    other = lax.ppermute(own, "gy", swap)
    out = f32(layers * parts * 2, columns)
    post_head, mix = call(
        update_kernel, (out, f32(parts, parts)), [SMEM] * 3 + [VMEM] * 3
    )(well_order, observed, variances, head_recv, own, other)
    post_perm = call(perm_kernel, out, [VMEM, VMEM])(perm_recv, mix)
    shape = (layers, parts, 2, columns)
    return post_perm.reshape(shape), post_head.reshape(shape)


def solution(mesh):
    placed = (P(None, "gx", None, "gy"), P(None, None, "gy"), P(), P(), P(), P())
    return jax.shard_map(
        body,
        mesh=mesh,
        in_specs=placed,
        out_specs=(P(None, None, "gx", "gy"), P(None, None, "gx", "gy")),
        check_vma=False,
    )
```

```python
import functools

import jax
import jax.numpy as jnp
from jax import lax
from jax.experimental import pallas as pl
from jax.experimental.pallas import tpu as pltpu
from jax.sharding import PartitionSpec as P

PASSES = 8
STEPS = 8
VERT = 0.1
LEAK = 0.1
PAD = 8
CHUNK = 32
HIGHEST = lax.Precision.HIGHEST

VMEM = pl.BlockSpec(memory_space=pltpu.VMEM)
SMEM = pl.BlockSpec(memory_space=pltpu.SMEM)
HBM = pl.BlockSpec(memory_space=pltpu.HBM)
PARAMS = pltpu.CompilerParams(vmem_limit_bytes=48 * 1024 * 1024)


def stage_kernel(perm_any, rech_any, perm_ref, rech_ref, sems):
    copies = []
    for which, (source, target) in enumerate(((perm_any, perm_ref), (rech_any, rech_ref))):
        for layer in range(source.shape[0]):
            copies.append(pltpu.make_async_copy(source.at[layer], target.at[layer], sems.at[which, layer]))
    for copy in copies:
        copy.start()
    for copy in copies:
        copy.wait()


def harmonic_inv(a, b):
    return 2.0 / (a + b)


def pack_rows(load, send_ref, layers, rows, stride):
    for half in range(2):
        for layer in range(layers):
            for r in range(2):
                row = 2 * layers * half + 2 * layer + r
                for g in range(0, rows // 2, 8):
                    send_ref[pl.ds(stride * g + row, 8, stride=stride), :] = load(half, layer, 2 * g + r)


def jacobi(perm, rech, send_ref, inv, rowt, vert, cn, cs, cw, ce, cu, cd, base, head_a, head_b):
    layers, rows, columns = perm[0].shape
    lane = lax.broadcasted_iota(jnp.int32, (CHUNK, columns), 1)
    west_end, east_end = lane == 0, lane == columns - 1
    ones = jnp.ones((PAD, columns), jnp.float32)
    zeros = jnp.zeros((PAD, columns), jnp.float32)
    for half in range(2):
        for layer in range(layers):
            inv[half, layer, 0:PAD, :] = ones
            inv[half, layer, PAD + rows:2 * PAD + rows, :] = ones
            for ref in (head_a, head_b):
                ref[half, layer, 0:PAD, :] = zeros
                ref[half, layer, PAD + rows:2 * PAD + rows, :] = zeros

    def chunks(work):
        for r in range(0, rows, CHUNK):
            work(r)

    def invert(r):
        for half in range(2):
            for layer in range(layers):
                inv[half, layer, pl.ds(PAD + r, CHUNK), :] = jnp.exp(-perm[half][layer, pl.ds(r, CHUNK), :])

    chunks(invert)
    for half in range(2):
        for layer in range(layers):
            rowt[half, layer, 0:PAD, :] = harmonic_inv(inv[half, layer, 0:PAD, :], inv[half, layer, 1:PAD + 1, :])

    def down(r):
        for half in range(2):
            for layer in range(layers):
                rowt[half, layer, pl.ds(PAD + r, CHUNK), :] = harmonic_inv(
                    inv[half, layer, pl.ds(PAD + r, CHUNK), :], inv[half, layer, pl.ds(PAD + r + 1, CHUNK), :]
                )

    chunks(down)

    def weigh(r):
        part = pl.ds(r, CHUNK)
        for layer in range(layers):
            left = inv[0, layer, pl.ds(PAD + r, CHUNK), :]
            right = inv[1, layer, pl.ds(PAD + r, CHUNK), :]
            left_e, right_e = pltpu.roll(left, columns - 1, 1), pltpu.roll(right, columns - 1, 1)
            east = [
                harmonic_inv(left, jnp.where(east_end, right_e, left_e)),
                harmonic_inv(right, jnp.where(east_end, 1.0, right_e)),
            ]
            left_w, right_w = pltpu.roll(east[0], 1, 1), pltpu.roll(east[1], 1, 1)
            west = [
                jnp.where(west_end, harmonic_inv(left, 1.0), left_w),
                jnp.where(west_end, left_w, right_w),
            ]
            for half, here in enumerate((left, right)):
                north = rowt[half, layer, pl.ds(PAD + r - 1, CHUNK), :]
                south = rowt[half, layer, pl.ds(PAD + r, CHUNK), :]
                diag = LEAK + north + south + west[half] + east[half]
                if layer > 0:
                    upper = vert[half, layer - 1, part, :]
                    diag = diag + upper
                if layer < layers - 1:
                    lower = VERT * harmonic_inv(here, inv[half, layer + 1, pl.ds(PAD + r, CHUNK), :])
                    vert[half, layer, part, :] = lower
                    diag = diag + lower
                scale = 1.0 / diag
                cn[half, layer, part, :] = north * scale
                cs[half, layer, part, :] = south * scale
                w, e = west[half] * scale, east[half] * scale
                cw[half, layer, part, :] = jnp.where(west_end, 0.0, w) if half == 0 else w
                ce[half, layer, part, :] = jnp.where(east_end, 0.0, e) if half == 1 else e
                if layer > 0:
                    cu[half, layer, part, :] = upper * scale
                if layer < layers - 1:
                    cd[half, layer, part, :] = lower * scale
                first = rech[half][layer, part, :] * scale
                base[half, layer, part, :] = first
                head_a[half, layer, pl.ds(PAD + r, CHUNK), :] = first

    chunks(weigh)

    def relax(old, new):
        def work(r):
            part = pl.ds(r, CHUNK)
            here = [[old[half, layer, pl.ds(PAD + r, CHUNK), :] for half in range(2)] for layer in range(layers)]
            for layer in range(layers):
                left, right = here[layer]
                left_w, right_w = pltpu.roll(left, 1, 1), pltpu.roll(right, 1, 1)
                left_e, right_e = pltpu.roll(left, columns - 1, 1), pltpu.roll(right, columns - 1, 1)
                west = [left_w, jnp.where(west_end, left_w, right_w)]
                east = [jnp.where(east_end, right_e, left_e), right_e]
                for half in range(2):
                    one = cn[half, layer, part, :] * old[half, layer, pl.ds(PAD + r - 1, CHUNK), :]
                    two = cs[half, layer, part, :] * old[half, layer, pl.ds(PAD + r + 1, CHUNK), :]
                    one = one + cw[half, layer, part, :] * west[half]
                    two = two + ce[half, layer, part, :] * east[half]
                    if layer > 0:
                        one = one + cu[half, layer, part, :] * here[layer - 1][half]
                    if layer < layers - 1:
                        two = two + cd[half, layer, part, :] * here[layer + 1][half]
                    new[half, layer, pl.ds(PAD + r, CHUNK), :] = base[half, layer, part, :] + one + two

        chunks(work)

    def two_passes(_, carry):
        relax(head_a, head_b)
        relax(head_b, head_a)
        return carry

    lax.fori_loop(0, (PASSES - 2) // 2, two_passes, 0)
    relax(head_a, head_b)
    last = head_b

    stride = send_ref.shape[0] * 2 // rows
    pack_rows(
        lambda half, layer, start: last[half, layer, pl.ds(PAD + start, 8, stride=2), :],
        send_ref, layers, rows, stride,
    )
    return last


def put_wells(last, cells_ref, order_ref, send_ref):
    rows, columns = last.shape[2] - 2 * PAD, last.shape[3]
    stride = send_ref.shape[0] * 2 // rows
    spot = lax.broadcasted_iota(jnp.int32, (1, columns), 1)
    wells = jnp.zeros((1, columns), jnp.float32)
    for k in range(STEPS):
        cell = cells_ref[order_ref[k]]
        width = 2 * columns
        line = last[cell % width // columns, cell // (rows * width), pl.ds(PAD + cell // width % rows, 1), :]
        moved = pltpu.roll(line, lax.rem(k - cell % columns + columns, columns), 1)
        wells = jnp.where(spot == k, moved, wells)
    block = jnp.broadcast_to(wells, (8, columns))
    for g in range(0, rows // 2, 8):
        send_ref[pl.ds(stride * g + stride - 1, 8, stride=stride), :] = block


def produce_kernel(
    core_ref, cells_any, order_any, perm_ref, rech_ref, perm_far, rech_far, send_ref,
    cells_ref, order_ref, sems, *scratch,
):
    layers, rows, columns = perm_ref.shape

    @pl.when(core_ref[0] == 0)
    def _():
        copies = [
            pltpu.make_async_copy(cells_any, cells_ref, sems.at[0]),
            pltpu.make_async_copy(order_any, order_ref, sems.at[1]),
        ]
        for copy in copies:
            copy.start()
        last = jacobi((perm_ref, perm_far), (rech_ref, rech_far), send_ref, *scratch)
        for copy in copies:
            copy.wait()
        put_wells(last, cells_ref, order_ref, send_ref)

    @pl.when(core_ref[0] == 1)
    def _():
        stride = send_ref.shape[0] * 2 // rows
        both = (perm_far, perm_ref)
        pack_rows(
            lambda half, layer, start: both[half][layer, pl.ds(start, 8, stride=2), :],
            send_ref, layers, rows, stride,
        )
        blank = jnp.zeros((8, columns), jnp.float32)
        for g in range(0, rows // 2, 8):
            send_ref[pl.ds(stride * g + stride - 1, 8, stride=stride), :] = blank


def split_kernel(core_ref, recv_ref, wells_ref, give_ref):
    members, stride = 128, recv_ref.shape[0] // 128
    wells_ref[...] = recv_ref[pl.ds(stride - 1, members, stride=stride), :].T[:STEPS]
    for core in range(2):
        @pl.when(core_ref[0] == core)
        def _():
            for j in range(8):
                give_ref[pl.ds(members * j, members), :] = recv_ref[
                    pl.ds(8 * (1 - core) + j, members, stride=stride), :
                ]


def steps_kernel(core_ref, order_ref, obs_ref, var_ref, own_ref, other_ref, mix_ref):
    members = own_ref.shape[1]
    y = jnp.where(core_ref[0] == 0, own_ref[...], other_ref[...])
    step_id = lax.broadcasted_iota(jnp.int32, y.shape, 0)
    means = jnp.sum(y, axis=1, keepdims=True) * (1.0 / members)
    spreads = y - means
    gains = jnp.zeros_like(y)
    weights_all = jnp.zeros_like(y)
    for k in range(STEPS):
        well = order_ref[k]
        spread = spreads[k:k + 1]
        variance = jnp.full((1, 1), var_ref[well], jnp.float32)
        products = jnp.sum(spreads * spread, axis=1, keepdims=True)
        denom = products[k:k + 1] / (members - 1) + variance
        alpha = 1.0 / (1.0 + jnp.sqrt(variance / denom))
        shift = obs_ref[well] - means[k:k + 1]
        weights = shift - alpha * spread
        factor = 1.0 / ((members - 1) * denom)
        earlier = jnp.sum(weights_all * spread, axis=1, keepdims=True)
        gain = factor * (spread + jnp.sum(gains * earlier, axis=0, keepdims=True))
        rate = factor * products
        means = means + rate * shift
        spreads = spreads - (rate * alpha) * spread
        gains = jnp.where(step_id == k, gain, gains)
        weights_all = jnp.where(step_id == k, weights, weights_all)
    mix_ref[...] = lax.dot_general(
        weights_all, gains, (((0,), (0,)), ((), ())), precision=HIGHEST,
        preferred_element_type=jnp.float32,
    )


def apply_kernel(core_ref, recv_ref, got_ref, mix_ref, perm_ref, head_ref):
    members, stride = 128, recv_ref.shape[0] // 128
    layer = pl.program_id(0)
    mix = mix_ref[...]

    def put(out_ref, r, x):
        out_ref[pl.ds(r, members, stride=2), :] = x + lax.dot_general(
            mix, x, (((1,), (0,)), ((), ())), precision=HIGHEST, preferred_element_type=jnp.float32
        )

    for core, kept, taken in ((0, head_ref, perm_ref), (1, perm_ref, head_ref)):
        @pl.when(core_ref[0] == core)
        def _():
            for r in range(2):
                row = 2 * layer + r
                put(kept, r, recv_ref[pl.ds(8 * core + row, members, stride=stride), :])
                put(taken, r, got_ref[pl.ds(pl.multiple_of(members * row, members), members), :])


def call(kernel, out, in_specs, scratch=()):
    return pl.pallas_call(
        kernel, out_shape=out, in_specs=in_specs,
        out_specs=jax.tree.map(lambda _: VMEM, out),
        scratch_shapes=list(scratch), compiler_params=PARAMS,
    )


def f32(*shape):
    return jax.ShapeDtypeStruct(shape, jnp.float32)


def produce(core, cells, order, perm, rech, perm_far, rech_far):
    layers, rows, columns = perm.shape
    field = pltpu.VMEM((2, layers, rows, columns), jnp.float32)
    padded = pltpu.VMEM((2, layers, rows + 2 * PAD, columns), jnp.float32)
    return call(
        produce_kernel, f32(rows // 2 * (4 * layers + 1), columns), [SMEM, HBM, HBM] + [VMEM] * 4,
        [pltpu.SMEM(cells.shape, jnp.int32), pltpu.SMEM(order.shape, jnp.int32), pltpu.SemaphoreType.DMA((2,))]
        + [padded, padded] + [field] * 8 + [padded, padded],
    )(core, cells, order, perm, rech, perm_far, rech_far)


def body(log_perm, recharge, well_cells, observed, variances, well_order):
    layers, _, rows, columns = log_perm.shape
    parts = lax.axis_size("gx")
    core = lax.axis_index("gy").astype(jnp.int32).reshape(1)
    swap = [(0, 1), (1, 0)]
    perm = log_perm.reshape(layers, rows, columns)
    perm_far = lax.ppermute(perm, "gy", swap)
    rech_far = lax.ppermute(recharge, "gy", swap)
    perm = pltpu.with_memory_space_constraint(perm, pltpu.HBM)
    recharge = pltpu.with_memory_space_constraint(recharge, pltpu.HBM)
    well_cells = pltpu.with_memory_space_constraint(well_cells, pltpu.HBM)
    well_order_any = pltpu.with_memory_space_constraint(well_order, pltpu.HBM)
    perm, recharge = call(
        stage_kernel, (f32(*perm.shape), f32(*recharge.shape)), [HBM, HBM], [pltpu.SemaphoreType.DMA((2, layers))]
    )(perm, recharge)
    send = produce(core, well_cells, well_order_any, perm, recharge, perm_far, rech_far)
    recv = lax.all_to_all(
        send.reshape(parts, -1, 1, columns), "gx", split_axis=0, concat_axis=0, tiled=True
    ).reshape(send.shape)
    own, give = call(
        split_kernel, (f32(STEPS, parts), f32(parts * 2 * layers, columns)), [SMEM, VMEM]
    )(core, recv)
    other = lax.ppermute(own, "gy", swap)
    other, give = lax.optimization_barrier((other, give))
    got = lax.ppermute(give, "gy", swap)
    mix = call(
        steps_kernel, f32(parts, parts), [SMEM] * 4 + [VMEM] * 2
    )(core, well_order, observed, variances, own, other)
    block = pl.BlockSpec((2 * parts, columns), lambda layer: (layer, 0))
    out = f32(layers * parts * 2, columns)
    post_perm, post_head = pl.pallas_call(
        apply_kernel, out_shape=(out, out), grid=(layers,),
        in_specs=[SMEM, VMEM, VMEM, VMEM], out_specs=(block, block), compiler_params=PARAMS,
    )(core, recv, got, mix)
    shape = (layers, parts, 2, columns)
    return post_perm.reshape(shape), post_head.reshape(shape)


def solution(mesh):
    placed = (P(None, "gx", None, "gy"), P(None, None, "gy"), P(), P(), P(), P())
    return jax.shard_map(
        body,
        mesh=mesh,
        in_specs=placed,
        out_specs=(P(None, None, "gx", "gy"), P(None, None, "gx", "gy")),
        check_vma=False,
    )
```

```python
import functools

import jax
import jax.numpy as jnp
from jax import lax
from jax.experimental import pallas as pl
from jax.experimental.pallas import tpu as pltpu
from jax.sharding import PartitionSpec as P

PASSES = 8
STEPS = 8
VERT = 0.1
LEAK = 0.1
PAD = 8
CHUNK = 32
HIGHEST = lax.Precision.HIGHEST

VMEM = pl.BlockSpec(memory_space=pltpu.VMEM)
SMEM = pl.BlockSpec(memory_space=pltpu.SMEM)
HBM = pl.BlockSpec(memory_space=pltpu.HBM)
PARAMS = pltpu.CompilerParams(vmem_limit_bytes=48 * 1024 * 1024)


def stage_kernel(
    perm_any, rech_any, order_any, obs_any, var_any, perm_ref, rech_ref, known_ref,
    order_ref, obs_ref, var_ref, sems, small_sems,
):
    small = [
        pltpu.make_async_copy(source, target, small_sems.at[which])
        for which, (source, target) in enumerate(
            ((order_any, order_ref), (obs_any, obs_ref), (var_any, var_ref))
        )
    ]
    copies = []
    for which, (source, target) in enumerate(((perm_any, perm_ref), (rech_any, rech_ref))):
        for layer in range(source.shape[0]):
            copies.append(pltpu.make_async_copy(source.at[layer], target.at[layer], sems.at[which, layer]))
    for copy in small + copies:
        copy.start()
    for copy in small:
        copy.wait()
    for k in range(STEPS):
        well = order_ref[k]
        known_ref[pl.ds(k, 1), :] = jnp.full((1, known_ref.shape[1]), obs_ref[well], jnp.float32)
        known_ref[pl.ds(STEPS + k, 1), :] = jnp.full((1, known_ref.shape[1]), var_ref[well], jnp.float32)
    for copy in copies:
        copy.wait()


def harmonic_inv(a, b):
    return 2.0 / (a + b)


def pack_rows(load, send_ref, layers, rows, stride):
    for half in range(2):
        for layer in range(layers):
            for r in range(2):
                row = 2 * layers * half + 2 * layer + r
                for g in range(0, rows // 2, 8):
                    send_ref[pl.ds(stride * g + row, 8, stride=stride), :] = load(half, layer, 2 * g + r)


def jacobi(perm, rech, send_ref, inv, rowt, vert, cn, cs, cw, ce, cu, cd, base, head_a, head_b):
    layers, rows, columns = perm[0].shape
    lane = lax.broadcasted_iota(jnp.int32, (CHUNK, columns), 1)
    west_end, east_end = lane == 0, lane == columns - 1
    ones = jnp.ones((PAD, columns), jnp.float32)
    zeros = jnp.zeros((PAD, columns), jnp.float32)
    for half in range(2):
        for layer in range(layers):
            inv[half, layer, 0:PAD, :] = ones
            inv[half, layer, PAD + rows:2 * PAD + rows, :] = ones
            for ref in (head_a, head_b):
                ref[half, layer, 0:PAD, :] = zeros
                ref[half, layer, PAD + rows:2 * PAD + rows, :] = zeros

    def chunks(work):
        for r in range(0, rows, CHUNK):
            work(r)

    def invert(r):
        for half in range(2):
            for layer in range(layers):
                inv[half, layer, pl.ds(PAD + r, CHUNK), :] = jnp.exp(-perm[half][layer, pl.ds(r, CHUNK), :])

    chunks(invert)
    for half in range(2):
        for layer in range(layers):
            rowt[half, layer, 0:PAD, :] = harmonic_inv(inv[half, layer, 0:PAD, :], inv[half, layer, 1:PAD + 1, :])

    def down(r):
        for half in range(2):
            for layer in range(layers):
                rowt[half, layer, pl.ds(PAD + r, CHUNK), :] = harmonic_inv(
                    inv[half, layer, pl.ds(PAD + r, CHUNK), :], inv[half, layer, pl.ds(PAD + r + 1, CHUNK), :]
                )

    chunks(down)

    def weigh(r):
        part = pl.ds(r, CHUNK)
        for layer in range(layers):
            left = inv[0, layer, pl.ds(PAD + r, CHUNK), :]
            right = inv[1, layer, pl.ds(PAD + r, CHUNK), :]
            left_e, right_e = pltpu.roll(left, columns - 1, 1), pltpu.roll(right, columns - 1, 1)
            east = [
                harmonic_inv(left, jnp.where(east_end, right_e, left_e)),
                harmonic_inv(right, jnp.where(east_end, 1.0, right_e)),
            ]
            left_w, right_w = pltpu.roll(east[0], 1, 1), pltpu.roll(east[1], 1, 1)
            west = [
                jnp.where(west_end, harmonic_inv(left, 1.0), left_w),
                jnp.where(west_end, left_w, right_w),
            ]
            for half, here in enumerate((left, right)):
                north = rowt[half, layer, pl.ds(PAD + r - 1, CHUNK), :]
                south = rowt[half, layer, pl.ds(PAD + r, CHUNK), :]
                diag = LEAK + north + south + west[half] + east[half]
                if layer > 0:
                    upper = vert[half, layer - 1, part, :]
                    diag = diag + upper
                if layer < layers - 1:
                    lower = VERT * harmonic_inv(here, inv[half, layer + 1, pl.ds(PAD + r, CHUNK), :])
                    vert[half, layer, part, :] = lower
                    diag = diag + lower
                scale = 1.0 / diag
                cn[half, layer, part, :] = north * scale
                cs[half, layer, part, :] = south * scale
                w, e = west[half] * scale, east[half] * scale
                cw[half, layer, part, :] = jnp.where(west_end, 0.0, w) if half == 0 else w
                ce[half, layer, part, :] = jnp.where(east_end, 0.0, e) if half == 1 else e
                if layer > 0:
                    cu[half, layer, part, :] = upper * scale
                if layer < layers - 1:
                    cd[half, layer, part, :] = lower * scale
                first = rech[half][layer, part, :] * scale
                base[half, layer, part, :] = first
                head_a[half, layer, pl.ds(PAD + r, CHUNK), :] = first

    chunks(weigh)

    def relax(old, new):
        def work(r):
            part = pl.ds(r, CHUNK)
            here = [[old[half, layer, pl.ds(PAD + r, CHUNK), :] for half in range(2)] for layer in range(layers)]
            for layer in range(layers):
                left, right = here[layer]
                left_w, right_w = pltpu.roll(left, 1, 1), pltpu.roll(right, 1, 1)
                left_e, right_e = pltpu.roll(left, columns - 1, 1), pltpu.roll(right, columns - 1, 1)
                west = [left_w, jnp.where(west_end, left_w, right_w)]
                east = [jnp.where(east_end, right_e, left_e), right_e]
                for half in range(2):
                    one = cn[half, layer, part, :] * old[half, layer, pl.ds(PAD + r - 1, CHUNK), :]
                    two = cs[half, layer, part, :] * old[half, layer, pl.ds(PAD + r + 1, CHUNK), :]
                    one = one + cw[half, layer, part, :] * west[half]
                    two = two + ce[half, layer, part, :] * east[half]
                    if layer > 0:
                        one = one + cu[half, layer, part, :] * here[layer - 1][half]
                    if layer < layers - 1:
                        two = two + cd[half, layer, part, :] * here[layer + 1][half]
                    new[half, layer, pl.ds(PAD + r, CHUNK), :] = base[half, layer, part, :] + one + two

        chunks(work)

    def two_passes(_, carry):
        relax(head_a, head_b)
        relax(head_b, head_a)
        return carry

    lax.fori_loop(0, (PASSES - 2) // 2, two_passes, 0)
    relax(head_a, head_b)
    last = head_b

    stride = send_ref.shape[0] * 2 // rows
    pack_rows(
        lambda half, layer, start: last[half, layer, pl.ds(PAD + start, 8, stride=2), :],
        send_ref, layers, rows, stride,
    )
    return last


def put_wells(last, cells_ref, order_ref, send_ref):
    rows, columns = last.shape[2] - 2 * PAD, last.shape[3]
    stride = send_ref.shape[0] * 2 // rows
    spot = lax.broadcasted_iota(jnp.int32, (1, columns), 1)
    wells = jnp.zeros((1, columns), jnp.float32)
    for k in range(STEPS):
        cell = cells_ref[order_ref[k]]
        width = 2 * columns
        line = last[cell % width // columns, cell // (rows * width), pl.ds(PAD + cell // width % rows, 1), :]
        moved = pltpu.roll(line, lax.rem(k - cell % columns + columns, columns), 1)
        wells = jnp.where(spot == k, moved, wells)
    block = jnp.broadcast_to(wells, (8, columns))
    for g in range(0, rows // 2, 8):
        send_ref[pl.ds(stride * g + stride - 1, 8, stride=stride), :] = block


def produce_kernel(
    core_ref, cells_any, order_any, perm_ref, rech_ref, perm_far, rech_far, send_ref,
    cells_ref, order_ref, sems, *scratch,
):
    layers, rows, columns = perm_ref.shape

    @pl.when(core_ref[0] == 0)
    def _():
        copies = [
            pltpu.make_async_copy(cells_any, cells_ref, sems.at[0]),
            pltpu.make_async_copy(order_any, order_ref, sems.at[1]),
        ]
        for copy in copies:
            copy.start()
        last = jacobi((perm_ref, perm_far), (rech_ref, rech_far), send_ref, *scratch)
        for copy in copies:
            copy.wait()
        put_wells(last, cells_ref, order_ref, send_ref)

    @pl.when(core_ref[0] == 1)
    def _():
        stride = send_ref.shape[0] * 2 // rows
        both = (perm_far, perm_ref)
        pack_rows(
            lambda half, layer, start: both[half][layer, pl.ds(start, 8, stride=2), :],
            send_ref, layers, rows, stride,
        )
        blank = jnp.zeros((8, columns), jnp.float32)
        for g in range(0, rows // 2, 8):
            send_ref[pl.ds(stride * g + stride - 1, 8, stride=stride), :] = blank


def wells_kernel(recv_ref, wells_ref):
    members, stride = 128, recv_ref.shape[0] // 128
    wells_ref[...] = recv_ref[pl.ds(stride - 1, members, stride=stride), :].T[:STEPS]


def give_kernel(core_ref, recv_ref, after_ref, give_ref):
    members, stride = 128, recv_ref.shape[0] // 128
    for j in range(8):
        give_ref[pl.ds(members * j, members), :] = recv_ref[
            pl.ds(8 * (1 - core_ref[0]) + j, members, stride=stride), :
        ]


def steps_kernel(known_ref, own_ref, mix_ref):
    members = own_ref.shape[1]
    y = own_ref[...]
    step_id = lax.broadcasted_iota(jnp.int32, y.shape, 0)
    means = jnp.sum(y, axis=1, keepdims=True) * (1.0 / members)
    spreads = y - means
    gains = jnp.zeros_like(y)
    weights_all = jnp.zeros_like(y)
    for k in range(STEPS):
        spread = spreads[k:k + 1]
        variance = known_ref[STEPS + k:STEPS + k + 1, :]
        products = jnp.sum(spreads * spread, axis=1, keepdims=True)
        denom = products[k:k + 1] / (members - 1) + variance
        alpha = 1.0 / (1.0 + jnp.sqrt(variance / denom))
        shift = known_ref[k:k + 1, :] - means[k:k + 1]
        weights = shift - alpha * spread
        factor = 1.0 / ((members - 1) * denom)
        earlier = jnp.sum(weights_all * spread, axis=1, keepdims=True)
        gain = factor * (spread + jnp.sum(gains * earlier, axis=0, keepdims=True))
        rate = factor * products
        means = means + rate * shift
        spreads = spreads - (rate * alpha) * spread
        gains = jnp.where(step_id == k, gain, gains)
        weights_all = jnp.where(step_id == k, weights, weights_all)
    mix_ref[...] = lax.dot_general(
        weights_all, gains, (((0,), (0,)), ((), ())), precision=HIGHEST,
        preferred_element_type=jnp.float32,
    )


def apply_kernel(core_ref, recv_ref, got_ref, own_mix_ref, other_mix_ref, perm_out, head_out, kept, taken, sems):
    members, stride = 128, recv_ref.shape[0] // 128
    layers = kept.shape[0]
    core = core_ref[0]
    mix = jnp.where(core == 0, own_mix_ref[...], other_mix_ref[...])
    mix_high, mix_low = split_bf16(mix)
    mixes = jnp.concatenate([mix_high, mix_high, mix_low], 1)

    def copies(own_out, got_out, layer):
        return [
            pltpu.make_async_copy(kept.at[layer], own_out.at[layer], sems.at[0, layer]),
            pltpu.make_async_copy(taken.at[layer], got_out.at[layer], sems.at[1, layer]),
        ]

    for layer in range(layers):
        x = jnp.concatenate(
            [recv_ref[pl.ds(8 * core + 2 * layer + r, members, stride=stride), :] for r in range(2)]
            + [got_ref[pl.ds(members * (2 * layer + r), members), :] for r in range(2)], 1
        )
        high, low = split_bf16(x)
        x = x + jnp.dot(
            mixes, jnp.concatenate([high, low, high], 0), preferred_element_type=jnp.float32
        )
        columns = x.shape[1] // 4
        for place, ref in enumerate((kept, taken)):
            for r in range(2):
                at = (2 * place + r) * columns
                ref[layer, pl.ds(r, members, stride=2), :] = x[:, at:at + columns]

        @pl.when(core == 0)
        def _():
            for copy in copies(head_out, perm_out, layer):
                copy.start()

        @pl.when(core == 1)
        def _():
            for copy in copies(perm_out, head_out, layer):
                copy.start()

    for layer in range(layers):
        for copy in copies(head_out, perm_out, layer):
            copy.wait()


def split_bf16(x):
    high = x.astype(jnp.bfloat16)
    return high, (x - high.astype(jnp.float32)).astype(jnp.bfloat16)


def call(kernel, out, in_specs, scratch=()):
    return pl.pallas_call(
        kernel, out_shape=out, in_specs=in_specs,
        out_specs=jax.tree.map(lambda _: VMEM, out),
        scratch_shapes=list(scratch), compiler_params=PARAMS,
    )


def f32(*shape):
    return jax.ShapeDtypeStruct(shape, jnp.float32)


def produce(core, cells, order, perm, rech, perm_far, rech_far):
    layers, rows, columns = perm.shape
    field = pltpu.VMEM((2, layers, rows, columns), jnp.float32)
    padded = pltpu.VMEM((2, layers, rows + 2 * PAD, columns), jnp.float32)
    return call(
        produce_kernel, f32(rows // 2 * (4 * layers + 1), columns), [SMEM, HBM, HBM] + [VMEM] * 4,
        [pltpu.SMEM(cells.shape, jnp.int32), pltpu.SMEM(order.shape, jnp.int32), pltpu.SemaphoreType.DMA((2,))]
        + [padded, padded] + [field] * 8 + [padded, padded],
    )(core, cells, order, perm, rech, perm_far, rech_far)


def body(log_perm, recharge, well_cells, observed, variances, well_order):
    layers, _, rows, columns = log_perm.shape
    parts = lax.axis_size("gx")
    core = lax.axis_index("gy").astype(jnp.int32).reshape(1)
    swap = [(0, 1), (1, 0)]
    perm = log_perm.reshape(layers, rows, columns)
    perm_far = lax.ppermute(perm, "gy", swap)
    rech_far = lax.ppermute(recharge, "gy", swap)
    perm, recharge, well_cells, well_order, observed, variances = (
        pltpu.with_memory_space_constraint(x, pltpu.HBM)
        for x in (perm, recharge, well_cells, well_order, observed, variances)
    )
    perm, recharge, known = call(
        stage_kernel, (f32(*perm.shape), f32(*recharge.shape), f32(2 * STEPS, parts)), [HBM] * 5,
        [pltpu.SMEM(well_order.shape, jnp.int32), pltpu.SMEM(observed.shape, jnp.float32)]
        + [pltpu.SMEM(variances.shape, jnp.float32), pltpu.SemaphoreType.DMA((2, layers))]
        + [pltpu.SemaphoreType.DMA((3,))],
    )(perm, recharge, well_order, observed, variances)
    send = produce(core, well_cells, well_order, perm, recharge, perm_far, rech_far)
    recv = lax.all_to_all(
        send.reshape(parts, -1, 1, columns), "gx", split_axis=0, concat_axis=0, tiled=True
    ).reshape(send.shape)
    own = call(wells_kernel, f32(STEPS, parts), [VMEM])(recv)
    give = call(give_kernel, f32(parts * 2 * layers, columns), [SMEM, VMEM, VMEM])(core, recv, own)
    got = lax.ppermute(give, "gy", swap)
    mix = call(
        steps_kernel, f32(parts, parts), [VMEM] * 2
    )(known, own)
    other_mix = lax.ppermute(mix, "gy", swap)
    field = (layers, parts * 2, columns)
    post_perm, post_head = pl.pallas_call(
        apply_kernel, out_shape=(f32(*field), f32(*field)),
        in_specs=[SMEM] + [VMEM] * 4, out_specs=(HBM, HBM),
        scratch_shapes=[pltpu.VMEM(field, jnp.float32)] * 2 + [pltpu.SemaphoreType.DMA((2, layers))],
        compiler_params=PARAMS,
    )(core, recv, got, mix, other_mix)
    shape = (layers, parts, 2, columns)
    return post_perm.reshape(shape), post_head.reshape(shape)


def solution(mesh):
    placed = (P(None, "gx", None, "gy"), P(None, None, "gy"), P(), P(), P(), P())
    return jax.shard_map(
        body,
        mesh=mesh,
        in_specs=placed,
        out_specs=(P(None, None, "gx", "gy"), P(None, None, "gx", "gy")),
        check_vma=False,
    )
```

```python
import functools

import jax
import jax.numpy as jnp
from jax import lax
from jax.experimental import pallas as pl
from jax.experimental.pallas import tpu as pltpu
from jax.sharding import PartitionSpec as P

PASSES = 8
STEPS = 8
VERT = 0.1
LEAK = 0.1
PAD = 8
CHUNK = 32
HIGHEST = lax.Precision.HIGHEST

VMEM = pl.BlockSpec(memory_space=pltpu.VMEM)
SMEM = pl.BlockSpec(memory_space=pltpu.SMEM)
HBM = pl.BlockSpec(memory_space=pltpu.HBM)
PARAMS = pltpu.CompilerParams(vmem_limit_bytes=48 * 1024 * 1024)


def stage_kernel(
    perm_any, rech_any, order_any, obs_any, var_any, perm_ref, rech_ref, known_ref,
    order_ref, obs_ref, var_ref, sems, small_sems,
):
    small = [
        pltpu.make_async_copy(source, target, small_sems.at[which])
        for which, (source, target) in enumerate(
            ((order_any, order_ref), (obs_any, obs_ref), (var_any, var_ref))
        )
    ]
    copies = []
    for which, (source, target) in enumerate(((perm_any, perm_ref), (rech_any, rech_ref))):
        for layer in range(source.shape[0]):
            copies.append(pltpu.make_async_copy(source.at[layer], target.at[layer], sems.at[which, layer]))
    for copy in small + copies:
        copy.start()
    for copy in small:
        copy.wait()
    for k in range(STEPS):
        well = order_ref[k]
        known_ref[pl.ds(k, 1), :] = jnp.full((1, known_ref.shape[1]), obs_ref[well], jnp.float32)
        known_ref[pl.ds(STEPS + k, 1), :] = jnp.full((1, known_ref.shape[1]), var_ref[well], jnp.float32)
    for copy in copies:
        copy.wait()


def harmonic_inv(a, b):
    return 2.0 / (a + b)


def pack_rows(load, send_ref, layers, rows, stride):
    for half in range(2):
        for layer in range(layers):
            for r in range(2):
                row = 2 * layers * half + 2 * layer + r
                for g in range(0, rows // 2, 8):
                    send_ref[pl.ds(stride * g + row, 8, stride=stride), :] = load(half, layer, 2 * g + r)


def jacobi(perm, rech, send_ref, inv, rowt, vert, cn, cs, cw, ce, cu, cd, base, head_a, head_b):
    layers, rows, columns = perm[0].shape
    lane = lax.broadcasted_iota(jnp.int32, (CHUNK, columns), 1)
    west_end, east_end = lane == 0, lane == columns - 1
    ones = jnp.ones((PAD, columns), jnp.float32)
    zeros = jnp.zeros((PAD, columns), jnp.float32)
    for half in range(2):
        for layer in range(layers):
            inv[half, layer, 0:PAD, :] = ones
            inv[half, layer, PAD + rows:2 * PAD + rows, :] = ones
            for ref in (head_a, head_b):
                ref[half, layer, 0:PAD, :] = zeros
                ref[half, layer, PAD + rows:2 * PAD + rows, :] = zeros

    def chunks(work):
        for r in range(0, rows, CHUNK):
            work(r)

    def invert(r):
        for half in range(2):
            for layer in range(layers):
                inv[half, layer, pl.ds(PAD + r, CHUNK), :] = jnp.exp(-perm[half][layer, pl.ds(r, CHUNK), :])

    chunks(invert)
    for half in range(2):
        for layer in range(layers):
            rowt[half, layer, 0:PAD, :] = harmonic_inv(inv[half, layer, 0:PAD, :], inv[half, layer, 1:PAD + 1, :])

    def down(r):
        for half in range(2):
            for layer in range(layers):
                rowt[half, layer, pl.ds(PAD + r, CHUNK), :] = harmonic_inv(
                    inv[half, layer, pl.ds(PAD + r, CHUNK), :], inv[half, layer, pl.ds(PAD + r + 1, CHUNK), :]
                )

    chunks(down)

    def weigh(r):
        part = pl.ds(r, CHUNK)
        for layer in range(layers):
            left = inv[0, layer, pl.ds(PAD + r, CHUNK), :]
            right = inv[1, layer, pl.ds(PAD + r, CHUNK), :]
            left_e, right_e = pltpu.roll(left, columns - 1, 1), pltpu.roll(right, columns - 1, 1)
            east = [
                harmonic_inv(left, jnp.where(east_end, right_e, left_e)),
                harmonic_inv(right, jnp.where(east_end, 1.0, right_e)),
            ]
            left_w, right_w = pltpu.roll(east[0], 1, 1), pltpu.roll(east[1], 1, 1)
            west = [
                jnp.where(west_end, harmonic_inv(left, 1.0), left_w),
                jnp.where(west_end, left_w, right_w),
            ]
            for half, here in enumerate((left, right)):
                north = rowt[half, layer, pl.ds(PAD + r - 1, CHUNK), :]
                south = rowt[half, layer, pl.ds(PAD + r, CHUNK), :]
                diag = LEAK + north + south + west[half] + east[half]
                if layer > 0:
                    upper = vert[half, layer - 1, part, :]
                    diag = diag + upper
                if layer < layers - 1:
                    lower = VERT * harmonic_inv(here, inv[half, layer + 1, pl.ds(PAD + r, CHUNK), :])
                    vert[half, layer, part, :] = lower
                    diag = diag + lower
                scale = 1.0 / diag
                cn[half, layer, part, :] = north * scale
                cs[half, layer, part, :] = south * scale
                w, e = west[half] * scale, east[half] * scale
                cw[half, layer, part, :] = jnp.where(west_end, 0.0, w) if half == 0 else w
                ce[half, layer, part, :] = jnp.where(east_end, 0.0, e) if half == 1 else e
                if layer > 0:
                    cu[half, layer, part, :] = upper * scale
                if layer < layers - 1:
                    cd[half, layer, part, :] = lower * scale
                first = rech[half][layer, part, :] * scale
                base[half, layer, part, :] = first
                head_a[half, layer, pl.ds(PAD + r, CHUNK), :] = first

    chunks(weigh)

    def relax(old, new):
        def work(r):
            part = pl.ds(r, CHUNK)
            here = [[old[half, layer, pl.ds(PAD + r, CHUNK), :] for half in range(2)] for layer in range(layers)]
            for layer in range(layers):
                left, right = here[layer]
                left_w, right_w = pltpu.roll(left, 1, 1), pltpu.roll(right, 1, 1)
                left_e, right_e = pltpu.roll(left, columns - 1, 1), pltpu.roll(right, columns - 1, 1)
                west = [left_w, jnp.where(west_end, left_w, right_w)]
                east = [jnp.where(east_end, right_e, left_e), right_e]
                for half in range(2):
                    one = cn[half, layer, part, :] * old[half, layer, pl.ds(PAD + r - 1, CHUNK), :]
                    two = cs[half, layer, part, :] * old[half, layer, pl.ds(PAD + r + 1, CHUNK), :]
                    one = one + cw[half, layer, part, :] * west[half]
                    two = two + ce[half, layer, part, :] * east[half]
                    if layer > 0:
                        one = one + cu[half, layer, part, :] * here[layer - 1][half]
                    if layer < layers - 1:
                        two = two + cd[half, layer, part, :] * here[layer + 1][half]
                    new[half, layer, pl.ds(PAD + r, CHUNK), :] = base[half, layer, part, :] + one + two

        chunks(work)

    def two_passes(_, carry):
        relax(head_a, head_b)
        relax(head_b, head_a)
        return carry

    lax.fori_loop(0, (PASSES - 2) // 2, two_passes, 0)
    relax(head_a, head_b)
    last = head_b

    stride = send_ref.shape[0] * 2 // rows
    pack_rows(
        lambda half, layer, start: last[half, layer, pl.ds(PAD + start, 8, stride=2), :],
        send_ref, layers, rows, stride,
    )
    return last


def put_wells(last, cells_ref, order_ref, send_ref):
    rows, columns = last.shape[2] - 2 * PAD, last.shape[3]
    stride = send_ref.shape[0] * 2 // rows
    spot = lax.broadcasted_iota(jnp.int32, (1, columns), 1)
    wells = jnp.zeros((1, columns), jnp.float32)
    for k in range(STEPS):
        cell = cells_ref[order_ref[k]]
        width = 2 * columns
        line = last[cell % width // columns, cell // (rows * width), pl.ds(PAD + cell // width % rows, 1), :]
        moved = pltpu.roll(line, lax.rem(k - cell % columns + columns, columns), 1)
        wells = jnp.where(spot == k, moved, wells)
    block = jnp.broadcast_to(wells, (8, columns))
    for g in range(0, rows // 2, 8):
        send_ref[pl.ds(stride * g + stride - 1, 8, stride=stride), :] = block


def produce_kernel(
    core_ref, cells_any, order_any, perm_ref, rech_ref, perm_far, rech_far, send_ref,
    cells_ref, order_ref, sems, *scratch,
):
    layers, rows, columns = perm_ref.shape

    @pl.when(core_ref[0] == 0)
    def _():
        copies = [
            pltpu.make_async_copy(cells_any, cells_ref, sems.at[0]),
            pltpu.make_async_copy(order_any, order_ref, sems.at[1]),
        ]
        for copy in copies:
            copy.start()
        last = jacobi((perm_ref, perm_far), (rech_ref, rech_far), send_ref, *scratch)
        for copy in copies:
            copy.wait()
        put_wells(last, cells_ref, order_ref, send_ref)

    @pl.when(core_ref[0] == 1)
    def _():
        stride = send_ref.shape[0] * 2 // rows
        both = (perm_far, perm_ref)
        pack_rows(
            lambda half, layer, start: both[half][layer, pl.ds(start, 8, stride=2), :],
            send_ref, layers, rows, stride,
        )
        blank = jnp.zeros((8, columns), jnp.float32)
        for g in range(0, rows // 2, 8):
            send_ref[pl.ds(stride * g + stride - 1, 8, stride=stride), :] = blank


def wells_kernel(recv_ref, wells_ref):
    members, stride = 128, recv_ref.shape[0] // 128
    wells_ref[...] = recv_ref[pl.ds(stride - 1, members, stride=stride), :].T[:STEPS]


def give_kernel(core_ref, recv_ref, after_ref, give_ref):
    members, stride = 128, recv_ref.shape[0] // 128
    for core in range(2):
        @pl.when(core_ref[0] == core)
        def _():
            for j in range(8):
                give_ref[pl.ds(members * j, members), :] = recv_ref[
                    pl.ds(8 * (1 - core) + j, members, stride=stride), :
                ]


def steps_kernel(known_ref, own_ref, mix_ref):
    members = own_ref.shape[1]
    y = own_ref[...]
    step_id = lax.broadcasted_iota(jnp.int32, y.shape, 0)
    means = jnp.sum(y, axis=1, keepdims=True) * (1.0 / members)
    spreads = y - means
    gains = jnp.zeros_like(y)
    weights_all = jnp.zeros_like(y)
    for k in range(STEPS):
        spread = spreads[k:k + 1]
        variance = known_ref[STEPS + k:STEPS + k + 1, :]
        products = jnp.sum(spreads * spread, axis=1, keepdims=True)
        denom = products[k:k + 1] / (members - 1) + variance
        alpha = 1.0 / (1.0 + jnp.sqrt(variance / denom))
        shift = known_ref[k:k + 1, :] - means[k:k + 1]
        weights = shift - alpha * spread
        factor = 1.0 / ((members - 1) * denom)
        earlier = jnp.sum(weights_all * spread, axis=1, keepdims=True)
        gain = factor * (spread + jnp.sum(gains * earlier, axis=0, keepdims=True))
        rate = factor * products
        means = means + rate * shift
        spreads = spreads - (rate * alpha) * spread
        gains = jnp.where(step_id == k, gain, gains)
        weights_all = jnp.where(step_id == k, weights, weights_all)
    mix_ref[...] = lax.dot_general(
        weights_all, gains, (((0,), (0,)), ((), ())), precision=HIGHEST,
        preferred_element_type=jnp.float32,
    )


def apply_kernel(core_ref, recv_ref, got_ref, own_mix_ref, other_mix_ref, perm_out, head_out, kept, taken, sems):
    members, stride = 128, recv_ref.shape[0] // 128
    layers = kept.shape[0]
    core = core_ref[0]
    mix = jnp.where(core == 0, own_mix_ref[...], other_mix_ref[...])
    mix_high, mix_low = split_bf16(mix)
    mixes = jnp.concatenate([mix_high, mix_high, mix_low], 1)

    def copies(own_out, got_out, layer):
        return [
            pltpu.make_async_copy(kept.at[layer], own_out.at[layer], sems.at[0, layer]),
            pltpu.make_async_copy(taken.at[layer], got_out.at[layer], sems.at[1, layer]),
        ]

    def run(first, own_out, got_out):
        for layer in range(layers):
            x = jnp.concatenate(
                [recv_ref[pl.ds(first + 2 * layer + r, members, stride=stride), :] for r in range(2)]
                + [got_ref[pl.ds(members * (2 * layer + r), members), :] for r in range(2)], 1
            )
            high, low = split_bf16(x)
            x = x + jnp.dot(
                mixes, jnp.concatenate([high, low, high], 0), preferred_element_type=jnp.float32
            )
            columns = x.shape[1] // 4
            for place, ref in enumerate((kept, taken)):
                for r in range(2):
                    at = (2 * place + r) * columns
                    ref[layer, pl.ds(r, members, stride=2), :] = x[:, at:at + columns]
            for copy in copies(own_out, got_out, layer):
                copy.start()
        for layer in range(layers):
            for copy in copies(own_out, got_out, layer):
                copy.wait()

    @pl.when(core == 0)
    def _():
        run(0, head_out, perm_out)

    @pl.when(core == 1)
    def _():
        run(8, perm_out, head_out)


def split_bf16(x):
    high = x.astype(jnp.bfloat16)
    return high, (x - high.astype(jnp.float32)).astype(jnp.bfloat16)


def call(kernel, out, in_specs, scratch=()):
    return pl.pallas_call(
        kernel, out_shape=out, in_specs=in_specs,
        out_specs=jax.tree.map(lambda _: VMEM, out),
        scratch_shapes=list(scratch), compiler_params=PARAMS,
    )


def f32(*shape):
    return jax.ShapeDtypeStruct(shape, jnp.float32)


def produce(core, cells, order, perm, rech, perm_far, rech_far):
    layers, rows, columns = perm.shape
    field = pltpu.VMEM((2, layers, rows, columns), jnp.float32)
    padded = pltpu.VMEM((2, layers, rows + 2 * PAD, columns), jnp.float32)
    return call(
        produce_kernel, f32(rows // 2 * (4 * layers + 1), columns), [SMEM, HBM, HBM] + [VMEM] * 4,
        [pltpu.SMEM(cells.shape, jnp.int32), pltpu.SMEM(order.shape, jnp.int32), pltpu.SemaphoreType.DMA((2,))]
        + [padded, padded] + [field] * 8 + [padded, padded],
    )(core, cells, order, perm, rech, perm_far, rech_far)


def body(log_perm, recharge, well_cells, observed, variances, well_order):
    layers, _, rows, columns = log_perm.shape
    parts = lax.axis_size("gx")
    core = lax.axis_index("gy").astype(jnp.int32).reshape(1)
    swap = [(0, 1), (1, 0)]
    perm = log_perm.reshape(layers, rows, columns)
    perm_far = lax.ppermute(perm, "gy", swap)
    rech_far = lax.ppermute(recharge, "gy", swap)
    perm, recharge, well_cells, well_order, observed, variances = (
        pltpu.with_memory_space_constraint(x, pltpu.HBM)
        for x in (perm, recharge, well_cells, well_order, observed, variances)
    )
    perm, recharge, known = call(
        stage_kernel, (f32(*perm.shape), f32(*recharge.shape), f32(2 * STEPS, parts)), [HBM] * 5,
        [pltpu.SMEM(well_order.shape, jnp.int32), pltpu.SMEM(observed.shape, jnp.float32)]
        + [pltpu.SMEM(variances.shape, jnp.float32), pltpu.SemaphoreType.DMA((2, layers))]
        + [pltpu.SemaphoreType.DMA((3,))],
    )(perm, recharge, well_order, observed, variances)
    send = produce(core, well_cells, well_order, perm, recharge, perm_far, rech_far)
    recv = lax.all_to_all(
        send.reshape(parts, -1, 1, columns), "gx", split_axis=0, concat_axis=0, tiled=True
    ).reshape(send.shape)
    own = call(wells_kernel, f32(STEPS, parts), [VMEM])(recv)
    give = call(give_kernel, f32(parts * 2 * layers, columns), [SMEM, VMEM, VMEM])(core, recv, own)
    got = lax.ppermute(give, "gy", swap)
    mix = call(
        steps_kernel, f32(parts, parts), [VMEM] * 2
    )(known, own)
    other_mix = lax.ppermute(mix, "gy", swap)
    field = (layers, parts * 2, columns)
    post_perm, post_head = pl.pallas_call(
        apply_kernel, out_shape=(f32(*field), f32(*field)),
        in_specs=[SMEM] + [VMEM] * 4, out_specs=(HBM, HBM),
        scratch_shapes=[pltpu.VMEM(field, jnp.float32)] * 2 + [pltpu.SemaphoreType.DMA((2, layers))],
        compiler_params=PARAMS,
    )(core, recv, got, mix, other_mix)
    shape = (layers, parts, 2, columns)
    return post_perm.reshape(shape), post_head.reshape(shape)


def solution(mesh):
    placed = (P(None, "gx", None, "gy"), P(None, None, "gy"), P(), P(), P(), P())
    return jax.shard_map(
        body,
        mesh=mesh,
        in_specs=placed,
        out_specs=(P(None, None, "gx", "gy"), P(None, None, "gx", "gy")),
        check_vma=False,
    )
```

```python
import functools

import jax
import jax.numpy as jnp
from jax import lax
from jax.experimental import pallas as pl
from jax.experimental.pallas import tpu as pltpu
from jax.sharding import PartitionSpec as P

PASSES = 8
STEPS = 8
VERT = 0.1
LEAK = 0.1
PAD = 8
CHUNK = 32
HIGHEST = lax.Precision.HIGHEST

VMEM = pl.BlockSpec(memory_space=pltpu.VMEM)
SMEM = pl.BlockSpec(memory_space=pltpu.SMEM)
HBM = pl.BlockSpec(memory_space=pltpu.HBM)
PARAMS = pltpu.CompilerParams(vmem_limit_bytes=48 * 1024 * 1024)


def stage_kernel(
    perm_any, rech_any, order_any, obs_any, var_any, perm_ref, rech_ref, known_ref,
    order_ref, obs_ref, var_ref, sems, small_sems,
):
    small = [
        pltpu.make_async_copy(source, target, small_sems.at[which])
        for which, (source, target) in enumerate(
            ((order_any, order_ref), (obs_any, obs_ref), (var_any, var_ref))
        )
    ]
    copies = []
    for which, (source, target) in enumerate(((perm_any, perm_ref), (rech_any, rech_ref))):
        for layer in range(source.shape[0]):
            copies.append(pltpu.make_async_copy(source.at[layer], target.at[layer], sems.at[which, layer]))
    for copy in small + copies:
        copy.start()
    for copy in small:
        copy.wait()
    for k in range(STEPS):
        well = order_ref[k]
        known_ref[pl.ds(k, 1), :] = jnp.full((1, known_ref.shape[1]), obs_ref[well], jnp.float32)
        known_ref[pl.ds(STEPS + k, 1), :] = jnp.full((1, known_ref.shape[1]), var_ref[well], jnp.float32)
    for copy in copies:
        copy.wait()


def harmonic_inv(a, b):
    return 2.0 / (a + b)


def pack_rows(load, send_ref, layers, rows, stride):
    for half in range(2):
        for layer in range(layers):
            for r in range(2):
                row = 2 * layers * half + 2 * layer + r
                for g in range(0, rows // 2, 8):
                    send_ref[pl.ds(stride * g + row, 8, stride=stride), :] = load(half, layer, 2 * g + r)


def jacobi(perm, rech, send_ref, inv, rowt, vert, cn, cs, cw, ce, cu, cd, base, head_a, head_b):
    layers, rows, columns = perm[0].shape
    lane = lax.broadcasted_iota(jnp.int32, (CHUNK, columns), 1)
    west_end, east_end = lane == 0, lane == columns - 1
    ones = jnp.ones((PAD, columns), jnp.float32)
    zeros = jnp.zeros((PAD, columns), jnp.float32)
    for half in range(2):
        for layer in range(layers):
            inv[half, layer, 0:PAD, :] = ones
            inv[half, layer, PAD + rows:2 * PAD + rows, :] = ones
            for ref in (head_a, head_b):
                ref[half, layer, 0:PAD, :] = zeros
                ref[half, layer, PAD + rows:2 * PAD + rows, :] = zeros

    def chunks(work):
        for r in range(0, rows, CHUNK):
            work(r)

    def invert(r):
        for half in range(2):
            for layer in range(layers):
                inv[half, layer, pl.ds(PAD + r, CHUNK), :] = jnp.exp(-perm[half][layer, pl.ds(r, CHUNK), :])

    chunks(invert)
    for half in range(2):
        for layer in range(layers):
            rowt[half, layer, 0:PAD, :] = harmonic_inv(inv[half, layer, 0:PAD, :], inv[half, layer, 1:PAD + 1, :])

    def down(r):
        for half in range(2):
            for layer in range(layers):
                rowt[half, layer, pl.ds(PAD + r, CHUNK), :] = harmonic_inv(
                    inv[half, layer, pl.ds(PAD + r, CHUNK), :], inv[half, layer, pl.ds(PAD + r + 1, CHUNK), :]
                )

    chunks(down)

    def weigh(r):
        part = pl.ds(r, CHUNK)
        for layer in range(layers):
            left = inv[0, layer, pl.ds(PAD + r, CHUNK), :]
            right = inv[1, layer, pl.ds(PAD + r, CHUNK), :]
            left_e, right_e = pltpu.roll(left, columns - 1, 1), pltpu.roll(right, columns - 1, 1)
            east = [
                harmonic_inv(left, jnp.where(east_end, right_e, left_e)),
                harmonic_inv(right, jnp.where(east_end, 1.0, right_e)),
            ]
            left_w, right_w = pltpu.roll(east[0], 1, 1), pltpu.roll(east[1], 1, 1)
            west = [
                jnp.where(west_end, harmonic_inv(left, 1.0), left_w),
                jnp.where(west_end, left_w, right_w),
            ]
            for half, here in enumerate((left, right)):
                north = rowt[half, layer, pl.ds(PAD + r - 1, CHUNK), :]
                south = rowt[half, layer, pl.ds(PAD + r, CHUNK), :]
                diag = LEAK + north + south + west[half] + east[half]
                if layer > 0:
                    upper = vert[half, layer - 1, part, :]
                    diag = diag + upper
                if layer < layers - 1:
                    lower = VERT * harmonic_inv(here, inv[half, layer + 1, pl.ds(PAD + r, CHUNK), :])
                    vert[half, layer, part, :] = lower
                    diag = diag + lower
                scale = 1.0 / diag
                cn[half, layer, part, :] = north * scale
                cs[half, layer, part, :] = south * scale
                w, e = west[half] * scale, east[half] * scale
                cw[half, layer, part, :] = jnp.where(west_end, 0.0, w) if half == 0 else w
                ce[half, layer, part, :] = jnp.where(east_end, 0.0, e) if half == 1 else e
                if layer > 0:
                    cu[half, layer, part, :] = upper * scale
                if layer < layers - 1:
                    cd[half, layer, part, :] = lower * scale
                first = rech[half][layer, part, :] * scale
                base[half, layer, part, :] = first
                head_a[half, layer, pl.ds(PAD + r, CHUNK), :] = first

    chunks(weigh)

    def relax(old, new):
        def work(r):
            part = pl.ds(r, CHUNK)
            here = [[old[half, layer, pl.ds(PAD + r, CHUNK), :] for half in range(2)] for layer in range(layers)]
            for layer in range(layers):
                left, right = here[layer]
                left_w, right_w = pltpu.roll(left, 1, 1), pltpu.roll(right, 1, 1)
                left_e, right_e = pltpu.roll(left, columns - 1, 1), pltpu.roll(right, columns - 1, 1)
                west = [left_w, jnp.where(west_end, left_w, right_w)]
                east = [jnp.where(east_end, right_e, left_e), right_e]
                for half in range(2):
                    one = cn[half, layer, part, :] * old[half, layer, pl.ds(PAD + r - 1, CHUNK), :]
                    two = cs[half, layer, part, :] * old[half, layer, pl.ds(PAD + r + 1, CHUNK), :]
                    one = one + cw[half, layer, part, :] * west[half]
                    two = two + ce[half, layer, part, :] * east[half]
                    if layer > 0:
                        one = one + cu[half, layer, part, :] * here[layer - 1][half]
                    if layer < layers - 1:
                        two = two + cd[half, layer, part, :] * here[layer + 1][half]
                    new[half, layer, pl.ds(PAD + r, CHUNK), :] = base[half, layer, part, :] + one + two

        chunks(work)

    def two_passes(_, carry):
        relax(head_a, head_b)
        relax(head_b, head_a)
        return carry

    lax.fori_loop(0, (PASSES - 2) // 2, two_passes, 0)
    relax(head_a, head_b)
    last = head_b

    stride = send_ref.shape[0] * 2 // rows
    pack_rows(
        lambda half, layer, start: last[half, layer, pl.ds(PAD + start, 8, stride=2), :],
        send_ref, layers, rows, stride,
    )
    return last


def put_wells(last, cells_ref, order_ref, send_ref):
    rows, columns = last.shape[2] - 2 * PAD, last.shape[3]
    stride = send_ref.shape[0] * 2 // rows
    spot = lax.broadcasted_iota(jnp.int32, (1, columns), 1)
    wells = jnp.zeros((1, columns), jnp.float32)
    for k in range(STEPS):
        cell = cells_ref[order_ref[k]]
        width = 2 * columns
        line = last[cell % width // columns, cell // (rows * width), pl.ds(PAD + cell // width % rows, 1), :]
        moved = pltpu.roll(line, lax.rem(k - cell % columns + columns, columns), 1)
        wells = jnp.where(spot == k, moved, wells)
    block = jnp.broadcast_to(wells, (8, columns))
    for g in range(0, rows // 2, 8):
        send_ref[pl.ds(stride * g + stride - 1, 8, stride=stride), :] = block


def heads_kernel(
    cells_any, order_any, perm_ref, rech_ref, perm_far, rech_far, send_ref,
    cells_ref, order_ref, sems, *scratch,
):
    copies = [
        pltpu.make_async_copy(cells_any, cells_ref, sems.at[0]),
        pltpu.make_async_copy(order_any, order_ref, sems.at[1]),
    ]
    for copy in copies:
        copy.start()
    last = jacobi((perm_ref, perm_far), (rech_ref, rech_far), send_ref, *scratch)
    for copy in copies:
        copy.wait()
    put_wells(last, cells_ref, order_ref, send_ref)


def pack_kernel(perm_ref, perm_far, send_ref):
    layers, rows, _ = perm_ref.shape
    both = (perm_far, perm_ref)
    pack_rows(
        lambda half, layer, start: both[half][layer, pl.ds(start, 8, stride=2), :],
        send_ref, layers, rows, 4 * layers,
    )


def wells_kernel(recv_ref, wells_ref):
    members, stride = 128, recv_ref.shape[0] // 128
    wells_ref[...] = recv_ref[pl.ds(stride - 1, members, stride=stride), :].T[:STEPS]


def give_kernel(core_ref, recv_ref, after_ref, give_ref):
    members, stride = 128, recv_ref.shape[0] // 128
    for core in range(2):
        @pl.when(core_ref[0] == core)
        def _():
            for j in range(8):
                give_ref[pl.ds(members * j, members), :] = recv_ref[
                    pl.ds(8 * (1 - core) + j, members, stride=stride - core), :
                ]


def steps_kernel(known_ref, own_ref, mix_ref):
    members = own_ref.shape[1]
    y = own_ref[...]
    step_id = lax.broadcasted_iota(jnp.int32, y.shape, 0)
    means = jnp.sum(y, axis=1, keepdims=True) * (1.0 / members)
    spreads = y - means
    gains = jnp.zeros_like(y)
    weights_all = jnp.zeros_like(y)
    for k in range(STEPS):
        spread = spreads[k:k + 1]
        variance = known_ref[STEPS + k:STEPS + k + 1, :]
        products = jnp.sum(spreads * spread, axis=1, keepdims=True)
        denom = products[k:k + 1] / (members - 1) + variance
        alpha = 1.0 / (1.0 + jnp.sqrt(variance / denom))
        shift = known_ref[k:k + 1, :] - means[k:k + 1]
        weights = shift - alpha * spread
        factor = 1.0 / ((members - 1) * denom)
        earlier = jnp.sum(weights_all * spread, axis=1, keepdims=True)
        gain = factor * (spread + jnp.sum(gains * earlier, axis=0, keepdims=True))
        rate = factor * products
        means = means + rate * shift
        spreads = spreads - (rate * alpha) * spread
        gains = jnp.where(step_id == k, gain, gains)
        weights_all = jnp.where(step_id == k, weights, weights_all)
    mix_ref[...] = lax.dot_general(
        weights_all, gains, (((0,), (0,)), ((), ())), precision=HIGHEST,
        preferred_element_type=jnp.float32,
    )


def apply_kernel(core_ref, recv_ref, got_ref, own_mix_ref, other_mix_ref, perm_out, head_out, kept, taken, sems):
    members, stride = 128, recv_ref.shape[0] // 128
    layers = kept.shape[0]
    core = core_ref[0]
    mix = jnp.where(core == 0, own_mix_ref[...], other_mix_ref[...])
    mix_high, mix_low = split_bf16(mix)
    mixes = jnp.concatenate([mix_high, mix_high, mix_low], 1)

    def copies(own_out, got_out, layer):
        return [
            pltpu.make_async_copy(kept.at[layer], own_out.at[layer], sems.at[0, layer]),
            pltpu.make_async_copy(taken.at[layer], got_out.at[layer], sems.at[1, layer]),
        ]

    def run(first, step, own_out, got_out):
        for layer in range(layers):
            x = jnp.concatenate(
                [recv_ref[pl.ds(first + 2 * layer + r, members, stride=step), :] for r in range(2)]
                + [got_ref[pl.ds(members * (2 * layer + r), members), :] for r in range(2)], 1
            )
            high, low = split_bf16(x)
            x = x + jnp.dot(
                mixes, jnp.concatenate([high, low, high], 0), preferred_element_type=jnp.float32
            )
            columns = x.shape[1] // 4
            for place, ref in enumerate((kept, taken)):
                for r in range(2):
                    at = (2 * place + r) * columns
                    ref[layer, pl.ds(r, members, stride=2), :] = x[:, at:at + columns]
            for copy in copies(own_out, got_out, layer):
                copy.start()
        for layer in range(layers):
            for copy in copies(own_out, got_out, layer):
                copy.wait()

    @pl.when(core == 0)
    def _():
        run(0, stride, head_out, perm_out)

    @pl.when(core == 1)
    def _():
        run(8, stride - 1, perm_out, head_out)


def split_bf16(x):
    high = x.astype(jnp.bfloat16)
    return high, (x - high.astype(jnp.float32)).astype(jnp.bfloat16)


def call(kernel, out, in_specs, scratch=()):
    return pl.pallas_call(
        kernel, out_shape=out, in_specs=in_specs,
        out_specs=jax.tree.map(lambda _: VMEM, out),
        scratch_shapes=list(scratch), compiler_params=PARAMS,
    )


def f32(*shape):
    return jax.ShapeDtypeStruct(shape, jnp.float32)


def exchange(send, parts):
    return lax.all_to_all(
        send.reshape(parts, -1, 1, send.shape[1]), "gx", split_axis=0, concat_axis=0, tiled=True
    ).reshape(send.shape)


def heads_part(cells, order, perm, rech, perm_far, rech_far, perm_recv):
    layers, rows, columns = perm.shape
    field = pltpu.VMEM((2, layers, rows, columns), jnp.float32)
    padded = pltpu.VMEM((2, layers, rows + 2 * PAD, columns), jnp.float32)
    send = call(
        heads_kernel, f32(rows // 2 * (4 * layers + 1), columns), [HBM, HBM] + [VMEM] * 4,
        [pltpu.SMEM(cells.shape, jnp.int32), pltpu.SMEM(order.shape, jnp.int32), pltpu.SemaphoreType.DMA((2,))]
        + [padded, padded] + [field] * 8 + [padded, padded],
    )(cells, order, perm, rech, perm_far, rech_far)
    return exchange(send, rows // 2)


def rest_part(cells, order, perm, rech, perm_far, rech_far, perm_recv):
    rows, columns = perm.shape[1:]
    return jnp.concatenate([perm_recv, jnp.zeros((rows // 2, columns), jnp.float32)], 0)


def perm_part(perm, perm_far):
    layers, rows, columns = perm.shape
    send = call(pack_kernel, f32(rows // 2 * 4 * layers, columns), [VMEM, VMEM])(perm, perm_far)
    return exchange(send, rows // 2)


def no_part(perm, perm_far):
    layers, rows, columns = perm.shape
    return jnp.zeros((rows // 2 * 4 * layers, columns), jnp.float32)


def body(log_perm, recharge, well_cells, observed, variances, well_order):
    layers, _, rows, columns = log_perm.shape
    parts = lax.axis_size("gx")
    core = lax.axis_index("gy").astype(jnp.int32).reshape(1)
    swap = [(0, 1), (1, 0)]
    perm = log_perm.reshape(layers, rows, columns)
    perm_far = lax.ppermute(perm, "gy", swap)
    rech_far = lax.ppermute(recharge, "gy", swap)
    perm, recharge, well_cells, well_order, observed, variances = (
        pltpu.with_memory_space_constraint(x, pltpu.HBM)
        for x in (perm, recharge, well_cells, well_order, observed, variances)
    )
    perm, recharge, known = call(
        stage_kernel, (f32(*perm.shape), f32(*recharge.shape), f32(2 * STEPS, parts)), [HBM] * 5,
        [pltpu.SMEM(well_order.shape, jnp.int32), pltpu.SMEM(observed.shape, jnp.float32)]
        + [pltpu.SMEM(variances.shape, jnp.float32), pltpu.SemaphoreType.DMA((2, layers))]
        + [pltpu.SemaphoreType.DMA((3,))],
    )(perm, recharge, well_order, observed, variances)
    perm_recv = lax.cond(core[0] == 1, perm_part, no_part, perm, perm_far)
    recv = lax.cond(
        core[0] == 0, heads_part, rest_part,
        well_cells, well_order, perm, recharge, perm_far, rech_far, perm_recv,
    )
    own = call(wells_kernel, f32(STEPS, parts), [VMEM])(recv)
    give = call(give_kernel, f32(parts * 2 * layers, columns), [SMEM, VMEM, VMEM])(core, recv, own)
    got = lax.ppermute(give, "gy", swap)
    mix = call(
        steps_kernel, f32(parts, parts), [VMEM] * 2
    )(known, own)
    other_mix = lax.ppermute(mix, "gy", swap)
    field = (layers, parts * 2, columns)
    post_perm, post_head = pl.pallas_call(
        apply_kernel, out_shape=(f32(*field), f32(*field)),
        in_specs=[SMEM] + [VMEM] * 4, out_specs=(HBM, HBM),
        scratch_shapes=[pltpu.VMEM(field, jnp.float32)] * 2 + [pltpu.SemaphoreType.DMA((2, layers))],
        compiler_params=PARAMS,
    )(core, recv, got, mix, other_mix)
    shape = (layers, parts, 2, columns)
    return post_perm.reshape(shape), post_head.reshape(shape)


def solution(mesh):
    placed = (P(None, "gx", None, "gy"), P(None, None, "gy"), P(), P(), P(), P())
    return jax.shard_map(
        body,
        mesh=mesh,
        in_specs=placed,
        out_specs=(P(None, None, "gx", "gy"), P(None, None, "gx", "gy")),
        check_vma=False,
    )
```

```python
import functools

import jax
import jax.numpy as jnp
from jax import lax
from jax.experimental import pallas as pl
from jax.experimental.pallas import tpu as pltpu
from jax.sharding import PartitionSpec as P

PASSES = 8
STEPS = 8
VERT = 0.1
LEAK = 0.1
PAD = 8
PLANE = 16
CHUNK = 32
HIGHEST = lax.Precision.HIGHEST

VMEM = pl.BlockSpec(memory_space=pltpu.VMEM)
SMEM = pl.BlockSpec(memory_space=pltpu.SMEM)
HBM = pl.BlockSpec(memory_space=pltpu.HBM)
PARAMS = pltpu.CompilerParams(vmem_limit_bytes=48 * 1024 * 1024)


def stage_kernel(
    perm_any, rech_any, order_any, obs_any, var_any, perm_ref, rech_ref, known_ref,
    order_ref, obs_ref, var_ref, sems, small_sems,
):
    small = [
        pltpu.make_async_copy(source, target, small_sems.at[which])
        for which, (source, target) in enumerate(
            ((order_any, order_ref), (obs_any, obs_ref), (var_any, var_ref))
        )
    ]
    copies = []
    for which, (source, target) in enumerate(((perm_any, perm_ref), (rech_any, rech_ref))):
        for layer in range(source.shape[0]):
            copies.append(pltpu.make_async_copy(source.at[layer], target.at[layer], sems.at[which, layer]))
    for copy in small + copies:
        copy.start()
    for copy in small:
        copy.wait()
    for k in range(STEPS):
        well = order_ref[k]
        known_ref[pl.ds(k, 1), :] = jnp.full((1, known_ref.shape[1]), obs_ref[well], jnp.float32)
        known_ref[pl.ds(STEPS + k, 1), :] = jnp.full((1, known_ref.shape[1]), var_ref[well], jnp.float32)
    for copy in copies:
        copy.wait()


def harmonic_inv(a, b):
    return 2.0 / (a + b)


def pack_rows(load, send_ref, layers, rows, stride):
    for half in range(2):
        for layer in range(layers):
            for r in range(2):
                row = 2 * layers * half + 2 * layer + r
                for g in range(0, rows // 2, 8):
                    send_ref[pl.ds(stride * g + row, 8, stride=stride), :] = load(half, layer, 2 * g + r)


def jacobi(perm, rech, send_ref, inv, rowt, vert, cn, cs, cw, ce, cu, cd, base, head_a, head_b):
    layers, rows, columns = perm[0].shape
    lane = lax.broadcasted_iota(jnp.int32, (CHUNK, columns), 1)
    west_end, east_end = lane == 0, lane == columns - 1
    ones = jnp.ones((PAD, columns), jnp.float32)
    zeros = jnp.zeros((PAD, columns), jnp.float32)
    for half in range(2):
        for layer in range(layers):
            inv[half, layer, 0:PAD, :] = ones
            inv[half, layer, PAD + rows:2 * PAD + rows, :] = ones
            for ref in (head_a, head_b):
                ref[half, layer, 0:PAD, :] = zeros
                ref[half, layer, PAD + rows:2 * PAD + rows, :] = zeros

    def chunks(work):
        for r in range(0, rows, CHUNK):
            work(r)

    def invert(r):
        for half in range(2):
            for layer in range(layers):
                inv[half, layer, pl.ds(PAD + r, CHUNK), :] = jnp.exp(-perm[half][layer, pl.ds(r, CHUNK), :])

    chunks(invert)
    for half in range(2):
        for layer in range(layers):
            rowt[half, layer, 0:PAD, :] = harmonic_inv(inv[half, layer, 0:PAD, :], inv[half, layer, 1:PAD + 1, :])

    def down(r):
        for half in range(2):
            for layer in range(layers):
                rowt[half, layer, pl.ds(PAD + r, CHUNK), :] = harmonic_inv(
                    inv[half, layer, pl.ds(PAD + r, CHUNK), :], inv[half, layer, pl.ds(PAD + r + 1, CHUNK), :]
                )

    chunks(down)

    def weigh(r):
        part = pl.ds(r, CHUNK)
        for layer in range(layers):
            left = inv[0, layer, pl.ds(PAD + r, CHUNK), :]
            right = inv[1, layer, pl.ds(PAD + r, CHUNK), :]
            left_e, right_e = pltpu.roll(left, columns - 1, 1), pltpu.roll(right, columns - 1, 1)
            east = [
                harmonic_inv(left, jnp.where(east_end, right_e, left_e)),
                harmonic_inv(right, jnp.where(east_end, 1.0, right_e)),
            ]
            left_w, right_w = pltpu.roll(east[0], 1, 1), pltpu.roll(east[1], 1, 1)
            west = [
                jnp.where(west_end, harmonic_inv(left, 1.0), left_w),
                jnp.where(west_end, left_w, right_w),
            ]
            for half, here in enumerate((left, right)):
                north = rowt[half, layer, pl.ds(PAD + r - 1, CHUNK), :]
                south = rowt[half, layer, pl.ds(PAD + r, CHUNK), :]
                diag = LEAK + north + south + west[half] + east[half]
                if layer > 0:
                    upper = vert[half, layer - 1, part, :]
                    diag = diag + upper
                if layer < layers - 1:
                    lower = VERT * harmonic_inv(here, inv[half, layer + 1, pl.ds(PAD + r, CHUNK), :])
                    vert[half, layer, part, :] = lower
                    diag = diag + lower
                scale = 1.0 / diag
                cn[half, layer, part, :] = north * scale
                cs[half, layer, part, :] = south * scale
                w, e = west[half] * scale, east[half] * scale
                cw[half, layer, part, :] = jnp.where(west_end, 0.0, w) if half == 0 else w
                ce[half, layer, part, :] = jnp.where(east_end, 0.0, e) if half == 1 else e
                if layer > 0:
                    cu[half, layer, part, :] = upper * scale
                if layer < layers - 1:
                    cd[half, layer, part, :] = lower * scale
                first = rech[half][layer, part, :] * scale
                base[half, layer, part, :] = first
                head_a[half, layer, pl.ds(PAD + r, CHUNK), :] = first

    chunks(weigh)

    def relax(old, new):
        def work(r):
            part = pl.ds(r, CHUNK)
            here = [[old[half, layer, pl.ds(PAD + r, CHUNK), :] for half in range(2)] for layer in range(layers)]
            for layer in range(layers):
                left, right = here[layer]
                left_w, right_w = pltpu.roll(left, 1, 1), pltpu.roll(right, 1, 1)
                left_e, right_e = pltpu.roll(left, columns - 1, 1), pltpu.roll(right, columns - 1, 1)
                west = [left_w, jnp.where(west_end, left_w, right_w)]
                east = [jnp.where(east_end, right_e, left_e), right_e]
                for half in range(2):
                    one = cn[half, layer, part, :] * old[half, layer, pl.ds(PAD + r - 1, CHUNK), :]
                    two = cs[half, layer, part, :] * old[half, layer, pl.ds(PAD + r + 1, CHUNK), :]
                    one = one + cw[half, layer, part, :] * west[half]
                    two = two + ce[half, layer, part, :] * east[half]
                    if layer > 0:
                        one = one + cu[half, layer, part, :] * here[layer - 1][half]
                    if layer < layers - 1:
                        two = two + cd[half, layer, part, :] * here[layer + 1][half]
                    new[half, layer, pl.ds(PAD + r, CHUNK), :] = base[half, layer, part, :] + one + two

        chunks(work)

    def two_passes(_, carry):
        relax(head_a, head_b)
        relax(head_b, head_a)
        return carry

    lax.fori_loop(0, (PASSES - 2) // 2, two_passes, 0)
    relax(head_a, head_b)
    last = head_b

    stride = send_ref.shape[0] * 2 // rows
    pack_rows(
        lambda half, layer, start: last[half, layer, pl.ds(PAD + start, 8, stride=2), :],
        send_ref, layers, rows, stride,
    )
    return last


def put_wells(last, cells_ref, order_ref, send_ref):
    rows, columns = last.shape[2] - 2 * PAD, last.shape[3]
    stride = send_ref.shape[0] * 2 // rows
    spot = lax.broadcasted_iota(jnp.int32, (1, columns), 1)
    wells = jnp.zeros((1, columns), jnp.float32)
    for k in range(STEPS):
        cell = cells_ref[order_ref[k]]
        width = 2 * columns
        line = last[cell % width // columns, cell // (rows * width), pl.ds(PAD + cell // width % rows, 1), :]
        moved = pltpu.roll(line, lax.rem(k - cell % columns + columns, columns), 1)
        wells = jnp.where(spot == k, moved, wells)
    block = jnp.broadcast_to(wells, (8, columns))
    for g in range(0, rows // 2, 8):
        send_ref[pl.ds(stride * g + stride - 1, 8, stride=stride), :] = block


def heads_kernel(
    cells_any, order_any, perm_ref, rech_ref, perm_far, rech_far, send_ref,
    cells_ref, order_ref, sems, *scratch,
):
    copies = [
        pltpu.make_async_copy(cells_any, cells_ref, sems.at[0]),
        pltpu.make_async_copy(order_any, order_ref, sems.at[1]),
    ]
    for copy in copies:
        copy.start()
    last = jacobi((perm_ref, perm_far), (rech_ref, rech_far), send_ref, *scratch)
    for copy in copies:
        copy.wait()
    put_wells(last, cells_ref, order_ref, send_ref)


def pack_kernel(perm_ref, perm_far, send_ref):
    layers, rows, _ = perm_ref.shape
    both = (perm_far, perm_ref)
    pack_rows(
        lambda half, layer, start: both[half][layer, pl.ds(start, 8, stride=2), :],
        send_ref, layers, rows, 4 * layers,
    )


def wells_kernel(recv_ref, wells_ref):
    members, stride = 128, recv_ref.shape[0] // 128
    wells_ref[...] = recv_ref[pl.ds(stride - 1, members, stride=stride), :].T[:STEPS]


def give_kernel(core_ref, recv_ref, after_ref, give_ref):
    members, stride = 128, recv_ref.shape[0] // 128
    for core in range(2):
        @pl.when(core_ref[0] == core)
        def _():
            for j in range(8):
                give_ref[pl.ds(members * j, members), :] = recv_ref[
                    pl.ds(8 * (1 - core) + j, members, stride=stride - core), :
                ]


def steps_kernel(known_ref, own_ref, mix_ref):
    members = own_ref.shape[1]
    y = own_ref[...]
    step_id = lax.broadcasted_iota(jnp.int32, y.shape, 0)
    means = jnp.sum(y, axis=1, keepdims=True) * (1.0 / members)
    spreads = y - means
    gains = jnp.zeros_like(y)
    weights_all = jnp.zeros_like(y)
    for k in range(STEPS):
        spread = spreads[k:k + 1]
        variance = known_ref[STEPS + k:STEPS + k + 1, :]
        products = jnp.sum(spreads * spread, axis=1, keepdims=True)
        denom = products[k:k + 1] / (members - 1) + variance
        alpha = 1.0 / (1.0 + jnp.sqrt(variance / denom))
        shift = known_ref[k:k + 1, :] - means[k:k + 1]
        weights = shift - alpha * spread
        factor = 1.0 / ((members - 1) * denom)
        earlier = jnp.sum(weights_all * spread, axis=1, keepdims=True)
        gain = factor * (spread + jnp.sum(gains * earlier, axis=0, keepdims=True))
        rate = factor * products
        means = means + rate * shift
        spreads = spreads - (rate * alpha) * spread
        gains = jnp.where(step_id == k, gain, gains)
        weights_all = jnp.where(step_id == k, weights, weights_all)
    mix_ref[...] = lax.dot_general(
        weights_all, gains, (((0,), (0,)), ((), ())), precision=HIGHEST,
        preferred_element_type=jnp.float32,
    )


def apply_kernel(core_ref, recv_ref, got_ref, own_mix_ref, other_mix_ref, perm_out, head_out, kept, taken, sems):
    members, stride = 128, recv_ref.shape[0] // 128
    layers = kept.shape[0]
    core = core_ref[0]
    mix = jnp.where(core == 0, own_mix_ref[...], other_mix_ref[...])
    mix_high, mix_low = split_bf16(mix)
    mixes = jnp.concatenate([mix_high, mix_high, mix_low], 1)

    def copies(own_out, got_out, layer):
        return [
            pltpu.make_async_copy(kept.at[layer], own_out.at[layer], sems.at[0, layer]),
            pltpu.make_async_copy(taken.at[layer], got_out.at[layer], sems.at[1, layer]),
        ]

    def run(first, step, own_out, got_out):
        for layer in range(layers):
            x = jnp.concatenate(
                [recv_ref[pl.ds(first + 2 * layer + r, members, stride=step), :] for r in range(2)]
                + [got_ref[pl.ds(members * (2 * layer + r), members), :] for r in range(2)], 1
            )
            high, low = split_bf16(x)
            x = x + jnp.dot(
                mixes, jnp.concatenate([high, low, high], 0), preferred_element_type=jnp.float32
            )
            columns = x.shape[1] // 4
            for place, ref in enumerate((kept, taken)):
                for r in range(2):
                    at = (2 * place + r) * columns
                    ref[layer, pl.ds(r, members, stride=2), :] = x[:, at:at + columns]
            for copy in copies(own_out, got_out, layer):
                copy.start()
        for layer in range(layers):
            for copy in copies(own_out, got_out, layer):
                copy.wait()

    @pl.when(core == 0)
    def _():
        run(0, stride, head_out, perm_out)

    @pl.when(core == 1)
    def _():
        run(8, stride - 1, perm_out, head_out)


def split_bf16(x):
    high = x.astype(jnp.bfloat16)
    return high, (x - high.astype(jnp.float32)).astype(jnp.bfloat16)


def call(kernel, out, in_specs, scratch=()):
    return pl.pallas_call(
        kernel, out_shape=out, in_specs=in_specs,
        out_specs=jax.tree.map(lambda _: VMEM, out),
        scratch_shapes=list(scratch), compiler_params=PARAMS,
    )


def f32(*shape):
    return jax.ShapeDtypeStruct(shape, jnp.float32)


def exchange(send, parts):
    return lax.all_to_all(
        send.reshape(parts, -1, 1, send.shape[1]), "gx", split_axis=0, concat_axis=0, tiled=True
    ).reshape(send.shape)


def heads_part(cells, order, perm, rech, perm_far, rech_far, perm_recv):
    layers, rows, columns = perm.shape
    field = pltpu.VMEM((2, layers, rows, columns), jnp.float32)
    padded = pltpu.VMEM((2, layers, rows + 2 * PAD, columns), jnp.float32)
    send = call(
        heads_kernel, f32(rows // 2 * (4 * layers + 1), columns), [HBM, HBM] + [VMEM] * 4,
        [pltpu.SMEM(cells.shape, jnp.int32), pltpu.SMEM(order.shape, jnp.int32), pltpu.SemaphoreType.DMA((2,))]
        + [padded, padded] + [field] * 8 + [padded, padded],
    )(cells, order, perm, rech, perm_far, rech_far)
    return exchange(send, rows // 2)


def rest_part(cells, order, perm, rech, perm_far, rech_far, perm_recv):
    rows, columns = perm.shape[1:]
    return jnp.concatenate([perm_recv, jnp.zeros((rows // 2, columns), jnp.float32)], 0)


def perm_part(perm, perm_far):
    layers, rows, columns = perm.shape
    send = call(pack_kernel, f32(rows // 2 * 4 * layers, columns), [VMEM, VMEM])(perm, perm_far)
    parts, depth = rows // 2, rows // 2 // PLANE
    along_z = [[z * PLANE + spot for z in range(depth)] for spot in range(PLANE)]
    in_plane = [[z * PLANE + spot for spot in range(PLANE)] for z in range(depth)]

    def stage(x, groups):
        return lax.all_to_all(
            x.reshape(parts, -1, 1, columns), "gx", split_axis=0, concat_axis=0, tiled=True,
            axis_index_groups=groups,
        )

    x = stage(send, along_z).reshape(depth, PLANE, -1, columns).swapaxes(0, 1)
    x = stage(x, in_plane).reshape(PLANE, depth, -1, columns).swapaxes(0, 1)
    return x.reshape(send.shape)


def no_part(perm, perm_far):
    layers, rows, columns = perm.shape
    return jnp.zeros((rows // 2 * 4 * layers, columns), jnp.float32)


def body(log_perm, recharge, well_cells, observed, variances, well_order):
    layers, _, rows, columns = log_perm.shape
    parts = lax.axis_size("gx")
    core = lax.axis_index("gy").astype(jnp.int32).reshape(1)
    swap = [(0, 1), (1, 0)]
    perm = log_perm.reshape(layers, rows, columns)
    perm_far = lax.ppermute(perm, "gy", swap)
    rech_far = lax.ppermute(recharge, "gy", swap)
    perm, recharge, well_cells, well_order, observed, variances = (
        pltpu.with_memory_space_constraint(x, pltpu.HBM)
        for x in (perm, recharge, well_cells, well_order, observed, variances)
    )
    perm, recharge, known = call(
        stage_kernel, (f32(*perm.shape), f32(*recharge.shape), f32(2 * STEPS, parts)), [HBM] * 5,
        [pltpu.SMEM(well_order.shape, jnp.int32), pltpu.SMEM(observed.shape, jnp.float32)]
        + [pltpu.SMEM(variances.shape, jnp.float32), pltpu.SemaphoreType.DMA((2, layers))]
        + [pltpu.SemaphoreType.DMA((3,))],
    )(perm, recharge, well_order, observed, variances)
    perm_recv = lax.cond(core[0] == 1, perm_part, no_part, perm, perm_far)
    recv = lax.cond(
        core[0] == 0, heads_part, rest_part,
        well_cells, well_order, perm, recharge, perm_far, rech_far, perm_recv,
    )
    own = call(wells_kernel, f32(STEPS, parts), [VMEM])(recv)
    give = call(give_kernel, f32(parts * 2 * layers, columns), [SMEM, VMEM, VMEM])(core, recv, own)
    got = lax.ppermute(give, "gy", swap)
    mix = call(
        steps_kernel, f32(parts, parts), [VMEM] * 2
    )(known, own)
    other_mix = lax.ppermute(mix, "gy", swap)
    field = (layers, parts * 2, columns)
    post_perm, post_head = pl.pallas_call(
        apply_kernel, out_shape=(f32(*field), f32(*field)),
        in_specs=[SMEM] + [VMEM] * 4, out_specs=(HBM, HBM),
        scratch_shapes=[pltpu.VMEM(field, jnp.float32)] * 2 + [pltpu.SemaphoreType.DMA((2, layers))],
        compiler_params=PARAMS,
    )(core, recv, got, mix, other_mix)
    shape = (layers, parts, 2, columns)
    return post_perm.reshape(shape), post_head.reshape(shape)


def solution(mesh):
    placed = (P(None, "gx", None, "gy"), P(None, None, "gy"), P(), P(), P(), P())
    return jax.shard_map(
        body,
        mesh=mesh,
        in_specs=placed,
        out_specs=(P(None, None, "gx", "gy"), P(None, None, "gx", "gy")),
        check_vma=False,
    )
```

```python
import functools

import jax
import jax.numpy as jnp
from jax import lax
from jax.experimental import pallas as pl
from jax.experimental.pallas import tpu as pltpu
from jax.sharding import PartitionSpec as P

PASSES = 8
STEPS = 8
VERT = 0.1
LEAK = 0.1
PAD = 8
PLANE = 16
CHUNK = 32
HIGHEST = lax.Precision.HIGHEST

VMEM = pl.BlockSpec(memory_space=pltpu.VMEM)
SMEM = pl.BlockSpec(memory_space=pltpu.SMEM)
HBM = pl.BlockSpec(memory_space=pltpu.HBM)
ANY = pl.BlockSpec(memory_space=pl.ANY)
PARAMS = pltpu.CompilerParams(vmem_limit_bytes=48 * 1024 * 1024)


def stage_kernel(
    perm_any, rech_any, order_any, obs_any, var_any, perm_ref, rech_ref, known_ref,
    order_ref, obs_ref, var_ref, sems, small_sems,
):
    small = [
        pltpu.make_async_copy(source, target, small_sems.at[which])
        for which, (source, target) in enumerate(
            ((order_any, order_ref), (obs_any, obs_ref), (var_any, var_ref))
        )
    ]
    copies = []
    for which, (source, target) in enumerate(((perm_any, perm_ref), (rech_any, rech_ref))):
        for layer in range(source.shape[0]):
            copies.append(pltpu.make_async_copy(source.at[layer], target.at[layer], sems.at[which, layer]))
    for copy in small + copies:
        copy.start()
    for copy in small:
        copy.wait()
    for k in range(STEPS):
        well = order_ref[k]
        known_ref[pl.ds(k, 1), :] = jnp.full((1, known_ref.shape[1]), obs_ref[well], jnp.float32)
        known_ref[pl.ds(STEPS + k, 1), :] = jnp.full((1, known_ref.shape[1]), var_ref[well], jnp.float32)
    for copy in copies:
        copy.wait()


def harmonic_inv(a, b):
    return 2.0 / (a + b)


def pack_rows(load, send_ref, layers, rows, stride):
    for half in range(2):
        for layer in range(layers):
            for r in range(2):
                row = 2 * layers * half + 2 * layer + r
                for g in range(0, rows // 2, 8):
                    send_ref[pl.ds(stride * g + row, 8, stride=stride), :] = load(half, layer, 2 * g + r)


def jacobi(perm, rech, rech_copy, send_ref, inv, rowt, vert, cn, cs, cw, ce, cu, cd, base, head_a, head_b):
    layers, rows, columns = perm[0].shape
    lane = lax.broadcasted_iota(jnp.int32, (CHUNK, columns), 1)
    west_end, east_end = lane == 0, lane == columns - 1
    ones = jnp.ones((PAD, columns), jnp.float32)
    zeros = jnp.zeros((PAD, columns), jnp.float32)
    for half in range(2):
        for layer in range(layers):
            inv[half, layer, 0:PAD, :] = ones
            inv[half, layer, PAD + rows:2 * PAD + rows, :] = ones
            for ref in (head_a, head_b):
                ref[half, layer, 0:PAD, :] = zeros
                ref[half, layer, PAD + rows:2 * PAD + rows, :] = zeros

    def chunks(work):
        for r in range(0, rows, CHUNK):
            work(r)

    def invert(r):
        for half in range(2):
            for layer in range(layers):
                inv[half, layer, pl.ds(PAD + r, CHUNK), :] = jnp.exp(-perm[half][layer, pl.ds(r, CHUNK), :])

    chunks(invert)
    for half in range(2):
        for layer in range(layers):
            rowt[half, layer, 0:PAD, :] = harmonic_inv(inv[half, layer, 0:PAD, :], inv[half, layer, 1:PAD + 1, :])

    def down(r):
        for half in range(2):
            for layer in range(layers):
                rowt[half, layer, pl.ds(PAD + r, CHUNK), :] = harmonic_inv(
                    inv[half, layer, pl.ds(PAD + r, CHUNK), :], inv[half, layer, pl.ds(PAD + r + 1, CHUNK), :]
                )

    chunks(down)

    def weigh(r):
        part = pl.ds(r, CHUNK)
        for layer in range(layers):
            left = inv[0, layer, pl.ds(PAD + r, CHUNK), :]
            right = inv[1, layer, pl.ds(PAD + r, CHUNK), :]
            left_e, right_e = pltpu.roll(left, columns - 1, 1), pltpu.roll(right, columns - 1, 1)
            east = [
                harmonic_inv(left, jnp.where(east_end, right_e, left_e)),
                harmonic_inv(right, jnp.where(east_end, 1.0, right_e)),
            ]
            left_w, right_w = pltpu.roll(east[0], 1, 1), pltpu.roll(east[1], 1, 1)
            west = [
                jnp.where(west_end, harmonic_inv(left, 1.0), left_w),
                jnp.where(west_end, left_w, right_w),
            ]
            for half, here in enumerate((left, right)):
                north = rowt[half, layer, pl.ds(PAD + r - 1, CHUNK), :]
                south = rowt[half, layer, pl.ds(PAD + r, CHUNK), :]
                diag = LEAK + north + south + west[half] + east[half]
                if layer > 0:
                    upper = vert[half, layer - 1, part, :]
                    diag = diag + upper
                if layer < layers - 1:
                    lower = VERT * harmonic_inv(here, inv[half, layer + 1, pl.ds(PAD + r, CHUNK), :])
                    vert[half, layer, part, :] = lower
                    diag = diag + lower
                scale = 1.0 / diag
                cn[half, layer, part, :] = north * scale
                cs[half, layer, part, :] = south * scale
                w, e = west[half] * scale, east[half] * scale
                cw[half, layer, part, :] = jnp.where(west_end, 0.0, w) if half == 0 else w
                ce[half, layer, part, :] = jnp.where(east_end, 0.0, e) if half == 1 else e
                if layer > 0:
                    cu[half, layer, part, :] = upper * scale
                if layer < layers - 1:
                    cd[half, layer, part, :] = lower * scale
                first = rech[half][layer, part, :] * scale
                base[half, layer, part, :] = first
                head_a[half, layer, pl.ds(PAD + r, CHUNK), :] = first

    rech_copy.wait()
    chunks(weigh)

    def relax(old, new):
        def work(r):
            part = pl.ds(r, CHUNK)
            here = [[old[half, layer, pl.ds(PAD + r, CHUNK), :] for half in range(2)] for layer in range(layers)]
            for layer in range(layers):
                left, right = here[layer]
                left_w, right_w = pltpu.roll(left, 1, 1), pltpu.roll(right, 1, 1)
                left_e, right_e = pltpu.roll(left, columns - 1, 1), pltpu.roll(right, columns - 1, 1)
                west = [left_w, jnp.where(west_end, left_w, right_w)]
                east = [jnp.where(east_end, right_e, left_e), right_e]
                for half in range(2):
                    one = cn[half, layer, part, :] * old[half, layer, pl.ds(PAD + r - 1, CHUNK), :]
                    two = cs[half, layer, part, :] * old[half, layer, pl.ds(PAD + r + 1, CHUNK), :]
                    one = one + cw[half, layer, part, :] * west[half]
                    two = two + ce[half, layer, part, :] * east[half]
                    if layer > 0:
                        one = one + cu[half, layer, part, :] * here[layer - 1][half]
                    if layer < layers - 1:
                        two = two + cd[half, layer, part, :] * here[layer + 1][half]
                    new[half, layer, pl.ds(PAD + r, CHUNK), :] = base[half, layer, part, :] + one + two

        chunks(work)

    def two_passes(_, carry):
        relax(head_a, head_b)
        relax(head_b, head_a)
        return carry

    lax.fori_loop(0, (PASSES - 2) // 2, two_passes, 0)
    relax(head_a, head_b)
    last = head_b

    stride = send_ref.shape[0] * 2 // rows
    pack_rows(
        lambda half, layer, start: last[half, layer, pl.ds(PAD + start, 8, stride=2), :],
        send_ref, layers, rows, stride,
    )
    return last


def put_wells(last, cells_ref, order_ref, send_ref):
    rows, columns = last.shape[2] - 2 * PAD, last.shape[3]
    stride = send_ref.shape[0] * 2 // rows
    spot = lax.broadcasted_iota(jnp.int32, (1, columns), 1)
    wells = jnp.zeros((1, columns), jnp.float32)
    for k in range(STEPS):
        cell = cells_ref[order_ref[k]]
        width = 2 * columns
        line = last[cell % width // columns, cell // (rows * width), pl.ds(PAD + cell // width % rows, 1), :]
        moved = pltpu.roll(line, lax.rem(k - cell % columns + columns, columns), 1)
        wells = jnp.where(spot == k, moved, wells)
    block = jnp.broadcast_to(wells, (8, columns))
    for g in range(0, rows // 2, 8):
        send_ref[pl.ds(stride * g + stride - 1, 8, stride=stride), :] = block


def heads_kernel(
    cells_any, order_any, perm_ref, rech_ref, perm_far, rech_any, send_ref,
    cells_ref, order_ref, rech_far, sems, *scratch,
):
    copies = [
        pltpu.make_async_copy(cells_any, cells_ref, sems.at[0]),
        pltpu.make_async_copy(order_any, order_ref, sems.at[1]),
    ]
    rech_copy = pltpu.make_async_copy(rech_any, rech_far, sems.at[2])
    rech_copy.start()
    for copy in copies:
        copy.start()
    last = jacobi((perm_ref, perm_far), (rech_ref, rech_far), rech_copy, send_ref, *scratch)
    for copy in copies:
        copy.wait()
    put_wells(last, cells_ref, order_ref, send_ref)


def pack_kernel(perm_ref, perm_far, send_ref):
    layers, rows, _ = perm_ref.shape
    both = (perm_far, perm_ref)
    pack_rows(
        lambda half, layer, start: both[half][layer, pl.ds(start, 8, stride=2), :],
        send_ref, layers, rows, 4 * layers,
    )


def wells_kernel(recv_ref, wells_ref):
    members, stride = 128, recv_ref.shape[0] // 128
    wells_ref[...] = recv_ref[pl.ds(stride - 1, members, stride=stride), :].T[:STEPS]


def give_kernel(core_ref, recv_ref, after_ref, give_ref):
    members, stride = 128, recv_ref.shape[0] // 128
    for core in range(2):
        @pl.when(core_ref[0] == core)
        def _():
            for j in range(8):
                give_ref[pl.ds(members * j, members), :] = recv_ref[
                    pl.ds(8 * (1 - core) + j, members, stride=stride - core), :
                ]


def steps_kernel(known_ref, own_ref, mix_ref):
    members = own_ref.shape[1]
    y = own_ref[...]
    step_id = lax.broadcasted_iota(jnp.int32, y.shape, 0)
    means = jnp.sum(y, axis=1, keepdims=True) * (1.0 / members)
    spreads = y - means
    gains = jnp.zeros_like(y)
    weights_all = jnp.zeros_like(y)
    for k in range(STEPS):
        spread = spreads[k:k + 1]
        variance = known_ref[STEPS + k:STEPS + k + 1, :]
        products = jnp.sum(spreads * spread, axis=1, keepdims=True)
        denom = products[k:k + 1] / (members - 1) + variance
        alpha = 1.0 / (1.0 + jnp.sqrt(variance / denom))
        shift = known_ref[k:k + 1, :] - means[k:k + 1]
        weights = shift - alpha * spread
        factor = 1.0 / ((members - 1) * denom)
        earlier = jnp.sum(weights_all * spread, axis=1, keepdims=True)
        gain = factor * (spread + jnp.sum(gains * earlier, axis=0, keepdims=True))
        rate = factor * products
        means = means + rate * shift
        spreads = spreads - (rate * alpha) * spread
        gains = jnp.where(step_id == k, gain, gains)
        weights_all = jnp.where(step_id == k, weights, weights_all)
    mix_ref[...] = lax.dot_general(
        weights_all, gains, (((0,), (0,)), ((), ())), precision=HIGHEST,
        preferred_element_type=jnp.float32,
    )


def apply_kernel(core_ref, recv_ref, got_ref, own_mix_ref, other_mix_ref, perm_out, head_out, kept, taken, sems):
    members, stride = 128, recv_ref.shape[0] // 128
    layers = kept.shape[0]
    core = core_ref[0]
    mix = jnp.where(core == 0, own_mix_ref[...], other_mix_ref[...])
    mix_high, mix_low = split_bf16(mix)
    mixes = jnp.concatenate([mix_high, mix_high, mix_low], 1)

    def copies(own_out, got_out, layer):
        return [
            pltpu.make_async_copy(kept.at[layer], own_out.at[layer], sems.at[0, layer]),
            pltpu.make_async_copy(taken.at[layer], got_out.at[layer], sems.at[1, layer]),
        ]

    def run(first, step, own_out, got_out):
        for layer in range(layers):
            x = jnp.concatenate(
                [recv_ref[pl.ds(first + 2 * layer + r, members, stride=step), :] for r in range(2)]
                + [got_ref[pl.ds(members * (2 * layer + r), members), :] for r in range(2)], 1
            )
            high, low = split_bf16(x)
            x = x + jnp.dot(
                mixes, jnp.concatenate([high, low, high], 0), preferred_element_type=jnp.float32
            )
            columns = x.shape[1] // 4
            for place, ref in enumerate((kept, taken)):
                for r in range(2):
                    at = (2 * place + r) * columns
                    ref[layer, pl.ds(r, members, stride=2), :] = x[:, at:at + columns]
            for copy in copies(own_out, got_out, layer):
                copy.start()
        for layer in range(layers):
            for copy in copies(own_out, got_out, layer):
                copy.wait()

    @pl.when(core == 0)
    def _():
        run(0, stride, head_out, perm_out)

    @pl.when(core == 1)
    def _():
        run(8, stride - 1, perm_out, head_out)


def split_bf16(x):
    high = x.astype(jnp.bfloat16)
    return high, (x - high.astype(jnp.float32)).astype(jnp.bfloat16)


def call(kernel, out, in_specs, scratch=()):
    return pl.pallas_call(
        kernel, out_shape=out, in_specs=in_specs,
        out_specs=jax.tree.map(lambda _: VMEM, out),
        scratch_shapes=list(scratch), compiler_params=PARAMS,
    )


def f32(*shape):
    return jax.ShapeDtypeStruct(shape, jnp.float32)


def exchange(send, parts):
    return lax.all_to_all(
        send.reshape(parts, -1, 1, send.shape[1]), "gx", split_axis=0, concat_axis=0, tiled=True
    ).reshape(send.shape)


def heads_part(cells, order, perm, rech, perm_far, rech_far, perm_recv):
    layers, rows, columns = perm.shape
    field = pltpu.VMEM((2, layers, rows, columns), jnp.float32)
    padded = pltpu.VMEM((2, layers, rows + 2 * PAD, columns), jnp.float32)
    send = call(
        heads_kernel, f32(rows // 2 * (4 * layers + 1), columns), [HBM, HBM] + [VMEM] * 3 + [ANY],
        [pltpu.SMEM(cells.shape, jnp.int32), pltpu.SMEM(order.shape, jnp.int32)]
        + [pltpu.VMEM(rech.shape, jnp.float32), pltpu.SemaphoreType.DMA((3,))]
        + [padded, padded] + [field] * 8 + [padded, padded],
    )(cells, order, perm, rech, perm_far, rech_far)
    return exchange(send, rows // 2)


def rest_part(cells, order, perm, rech, perm_far, rech_far, perm_recv):
    rows, columns = perm.shape[1:]
    return jnp.concatenate([perm_recv, jnp.zeros((rows // 2, columns), jnp.float32)], 0)


def perm_part(perm, perm_far):
    layers, rows, columns = perm.shape
    send = call(pack_kernel, f32(rows // 2 * 4 * layers, columns), [VMEM, VMEM])(perm, perm_far)
    parts, depth = rows // 2, rows // 2 // PLANE
    along_z = [[z * PLANE + spot for z in range(depth)] for spot in range(PLANE)]
    in_plane = [[z * PLANE + spot for spot in range(PLANE)] for z in range(depth)]

    def stage(x, groups):
        return lax.all_to_all(
            x.reshape(parts, -1, 1, columns), "gx", split_axis=0, concat_axis=0, tiled=True,
            axis_index_groups=groups,
        )

    x = stage(send, along_z).reshape(depth, PLANE, -1, columns).swapaxes(0, 1)
    x = stage(x, in_plane).reshape(PLANE, depth, -1, columns).swapaxes(0, 1)
    return x.reshape(send.shape)


def no_part(perm, perm_far):
    layers, rows, columns = perm.shape
    return jnp.zeros((rows // 2 * 4 * layers, columns), jnp.float32)


def body(log_perm, recharge, well_cells, observed, variances, well_order):
    layers, _, rows, columns = log_perm.shape
    parts = lax.axis_size("gx")
    core = lax.axis_index("gy").astype(jnp.int32).reshape(1)
    swap = [(0, 1), (1, 0)]
    perm = log_perm.reshape(layers, rows, columns)
    perm_far = lax.ppermute(perm, "gy", swap)
    rech_far = lax.ppermute(recharge, "gy", swap)
    perm, recharge, well_cells, well_order, observed, variances = (
        pltpu.with_memory_space_constraint(x, pltpu.HBM)
        for x in (perm, recharge, well_cells, well_order, observed, variances)
    )
    perm, recharge, known = call(
        stage_kernel, (f32(*perm.shape), f32(*recharge.shape), f32(2 * STEPS, parts)), [HBM] * 5,
        [pltpu.SMEM(well_order.shape, jnp.int32), pltpu.SMEM(observed.shape, jnp.float32)]
        + [pltpu.SMEM(variances.shape, jnp.float32), pltpu.SemaphoreType.DMA((2, layers))]
        + [pltpu.SemaphoreType.DMA((3,))],
    )(perm, recharge, well_order, observed, variances)
    perm_recv = lax.cond(core[0] == 1, perm_part, no_part, perm, perm_far)
    recv = lax.cond(
        core[0] == 0, heads_part, rest_part,
        well_cells, well_order, perm, recharge, perm_far, rech_far, perm_recv,
    )
    own = call(wells_kernel, f32(STEPS, parts), [VMEM])(recv)
    give = call(give_kernel, f32(parts * 2 * layers, columns), [SMEM, VMEM, VMEM])(core, recv, own)
    got = lax.ppermute(give, "gy", swap)
    mix = call(
        steps_kernel, f32(parts, parts), [VMEM] * 2
    )(known, own)
    other_mix = lax.ppermute(mix, "gy", swap)
    field = (layers, parts * 2, columns)
    post_perm, post_head = pl.pallas_call(
        apply_kernel, out_shape=(f32(*field), f32(*field)),
        in_specs=[SMEM] + [VMEM] * 4, out_specs=(HBM, HBM),
        scratch_shapes=[pltpu.VMEM(field, jnp.float32)] * 2 + [pltpu.SemaphoreType.DMA((2, layers))],
        compiler_params=PARAMS,
    )(core, recv, got, mix, other_mix)
    shape = (layers, parts, 2, columns)
    return post_perm.reshape(shape), post_head.reshape(shape)


def solution(mesh):
    placed = (P(None, "gx", None, "gy"), P(None, None, "gy"), P(), P(), P(), P())
    return jax.shard_map(
        body,
        mesh=mesh,
        in_specs=placed,
        out_specs=(P(None, None, "gx", "gy"), P(None, None, "gx", "gy")),
        check_vma=False,
    )
```

```python
import functools

import jax
import jax.numpy as jnp
from jax import lax
from jax.experimental import pallas as pl
from jax.experimental.pallas import tpu as pltpu
from jax.sharding import PartitionSpec as P

PASSES = 8
STEPS = 8
VERT = 0.1
LEAK = 0.1
PAD = 8
PLANE = 16
CHUNK = 64
HIGHEST = lax.Precision.HIGHEST

VMEM = pl.BlockSpec(memory_space=pltpu.VMEM)
SMEM = pl.BlockSpec(memory_space=pltpu.SMEM)
HBM = pl.BlockSpec(memory_space=pltpu.HBM)
PARAMS = pltpu.CompilerParams(vmem_limit_bytes=48 * 1024 * 1024)


def stage_kernel(
    perm_any, rech_any, order_any, obs_any, var_any, perm_ref, rech_ref, known_ref,
    order_ref, obs_ref, var_ref, sems, small_sems,
):
    small = [
        pltpu.make_async_copy(source, target, small_sems.at[which])
        for which, (source, target) in enumerate(
            ((order_any, order_ref), (obs_any, obs_ref), (var_any, var_ref))
        )
    ]
    copies = []
    for which, (source, target) in enumerate(((perm_any, perm_ref), (rech_any, rech_ref))):
        for layer in range(source.shape[0]):
            copies.append(pltpu.make_async_copy(source.at[layer], target.at[layer], sems.at[which, layer]))
    for copy in small + copies:
        copy.start()
    for copy in small:
        copy.wait()
    for k in range(STEPS):
        well = order_ref[k]
        known_ref[pl.ds(k, 1), :] = jnp.full((1, known_ref.shape[1]), obs_ref[well], jnp.float32)
        known_ref[pl.ds(STEPS + k, 1), :] = jnp.full((1, known_ref.shape[1]), var_ref[well], jnp.float32)
    for copy in copies:
        copy.wait()


def harmonic_inv(a, b):
    return 2.0 / (a + b)


def pack_rows(load, send_ref, layers, rows, stride):
    for half in range(2):
        for layer in range(layers):
            for r in range(2):
                row = 2 * layers * half + 2 * layer + r
                for g in range(0, rows // 2, 8):
                    send_ref[pl.ds(stride * g + row, 8, stride=stride), :] = load(half, layer, 2 * g + r)


def jacobi(perm, rech, send_ref, inv, rowt, vert, cn, cs, cw, ce, cu, cd, base, head_a, head_b):
    layers, rows, columns = perm[0].shape
    lane = lax.broadcasted_iota(jnp.int32, (CHUNK, columns), 1)
    west_end, east_end = lane == 0, lane == columns - 1
    ones = jnp.ones((PAD, columns), jnp.float32)
    zeros = jnp.zeros((PAD, columns), jnp.float32)
    for half in range(2):
        for layer in range(layers):
            inv[half, layer, 0:PAD, :] = ones
            inv[half, layer, PAD + rows:2 * PAD + rows, :] = ones
            for ref in (head_a, head_b):
                ref[half, layer, 0:PAD, :] = zeros
                ref[half, layer, PAD + rows:2 * PAD + rows, :] = zeros

    def chunks(work):
        for r in range(0, rows, CHUNK):
            work(r)

    def invert(r):
        for half in range(2):
            for layer in range(layers):
                inv[half, layer, pl.ds(PAD + r, CHUNK), :] = jnp.exp(-perm[half][layer, pl.ds(r, CHUNK), :])

    chunks(invert)
    for half in range(2):
        for layer in range(layers):
            rowt[half, layer, 0:PAD, :] = harmonic_inv(inv[half, layer, 0:PAD, :], inv[half, layer, 1:PAD + 1, :])

    def down(r):
        for half in range(2):
            for layer in range(layers):
                rowt[half, layer, pl.ds(PAD + r, CHUNK), :] = harmonic_inv(
                    inv[half, layer, pl.ds(PAD + r, CHUNK), :], inv[half, layer, pl.ds(PAD + r + 1, CHUNK), :]
                )

    chunks(down)

    def weigh(r):
        part = pl.ds(r, CHUNK)
        for layer in range(layers):
            left = inv[0, layer, pl.ds(PAD + r, CHUNK), :]
            right = inv[1, layer, pl.ds(PAD + r, CHUNK), :]
            left_e, right_e = pltpu.roll(left, columns - 1, 1), pltpu.roll(right, columns - 1, 1)
            east = [
                harmonic_inv(left, jnp.where(east_end, right_e, left_e)),
                harmonic_inv(right, jnp.where(east_end, 1.0, right_e)),
            ]
            left_w, right_w = pltpu.roll(east[0], 1, 1), pltpu.roll(east[1], 1, 1)
            west = [
                jnp.where(west_end, harmonic_inv(left, 1.0), left_w),
                jnp.where(west_end, left_w, right_w),
            ]
            for half, here in enumerate((left, right)):
                north = rowt[half, layer, pl.ds(PAD + r - 1, CHUNK), :]
                south = rowt[half, layer, pl.ds(PAD + r, CHUNK), :]
                diag = LEAK + north + south + west[half] + east[half]
                if layer > 0:
                    upper = vert[half, layer - 1, part, :]
                    diag = diag + upper
                if layer < layers - 1:
                    lower = VERT * harmonic_inv(here, inv[half, layer + 1, pl.ds(PAD + r, CHUNK), :])
                    vert[half, layer, part, :] = lower
                    diag = diag + lower
                scale = 1.0 / diag
                cn[half, layer, part, :] = north * scale
                cs[half, layer, part, :] = south * scale
                w, e = west[half] * scale, east[half] * scale
                cw[half, layer, part, :] = jnp.where(west_end, 0.0, w) if half == 0 else w
                ce[half, layer, part, :] = jnp.where(east_end, 0.0, e) if half == 1 else e
                if layer > 0:
                    cu[half, layer, part, :] = upper * scale
                if layer < layers - 1:
                    cd[half, layer, part, :] = lower * scale
                first = rech[half][layer, part, :] * scale
                base[half, layer, part, :] = first
                head_a[half, layer, pl.ds(PAD + r, CHUNK), :] = first

    chunks(weigh)

    def relax(old, new):
        def work(r):
            part = pl.ds(r, CHUNK)
            here = [[old[half, layer, pl.ds(PAD + r, CHUNK), :] for half in range(2)] for layer in range(layers)]
            for layer in range(layers):
                left, right = here[layer]
                left_w, right_w = pltpu.roll(left, 1, 1), pltpu.roll(right, 1, 1)
                left_e, right_e = pltpu.roll(left, columns - 1, 1), pltpu.roll(right, columns - 1, 1)
                west = [left_w, jnp.where(west_end, left_w, right_w)]
                east = [jnp.where(east_end, right_e, left_e), right_e]
                for half in range(2):
                    one = cn[half, layer, part, :] * old[half, layer, pl.ds(PAD + r - 1, CHUNK), :]
                    two = cs[half, layer, part, :] * old[half, layer, pl.ds(PAD + r + 1, CHUNK), :]
                    one = one + cw[half, layer, part, :] * west[half]
                    two = two + ce[half, layer, part, :] * east[half]
                    if layer > 0:
                        one = one + cu[half, layer, part, :] * here[layer - 1][half]
                    if layer < layers - 1:
                        two = two + cd[half, layer, part, :] * here[layer + 1][half]
                    new[half, layer, pl.ds(PAD + r, CHUNK), :] = base[half, layer, part, :] + one + two

        chunks(work)

    def two_passes(_, carry):
        relax(head_a, head_b)
        relax(head_b, head_a)
        return carry

    lax.fori_loop(0, (PASSES - 2) // 2, two_passes, 0)
    relax(head_a, head_b)
    last = head_b

    stride = send_ref.shape[0] * 2 // rows
    pack_rows(
        lambda half, layer, start: last[half, layer, pl.ds(PAD + start, 8, stride=2), :],
        send_ref, layers, rows, stride,
    )
    return last


def put_wells(last, cells_ref, order_ref, send_ref):
    rows, columns = last.shape[2] - 2 * PAD, last.shape[3]
    stride = send_ref.shape[0] * 2 // rows
    spot = lax.broadcasted_iota(jnp.int32, (1, columns), 1)
    wells = jnp.zeros((1, columns), jnp.float32)
    for k in range(STEPS):
        cell = cells_ref[order_ref[k]]
        width = 2 * columns
        line = last[cell % width // columns, cell // (rows * width), pl.ds(PAD + cell // width % rows, 1), :]
        moved = pltpu.roll(line, lax.rem(k - cell % columns + columns, columns), 1)
        wells = jnp.where(spot == k, moved, wells)
    block = jnp.broadcast_to(wells, (8, columns))
    for g in range(0, rows // 2, 8):
        send_ref[pl.ds(stride * g + stride - 1, 8, stride=stride), :] = block


def heads_kernel(
    cells_any, order_any, perm_ref, rech_ref, perm_far, rech_far, send_ref,
    cells_ref, order_ref, sems, *scratch,
):
    copies = [
        pltpu.make_async_copy(cells_any, cells_ref, sems.at[0]),
        pltpu.make_async_copy(order_any, order_ref, sems.at[1]),
    ]
    for copy in copies:
        copy.start()
    last = jacobi((perm_ref, perm_far), (rech_ref, rech_far), send_ref, *scratch)
    for copy in copies:
        copy.wait()
    put_wells(last, cells_ref, order_ref, send_ref)


def pack_kernel(perm_ref, perm_far, send_ref):
    layers, rows, _ = perm_ref.shape
    both = (perm_far, perm_ref)
    pack_rows(
        lambda half, layer, start: both[half][layer, pl.ds(start, 8, stride=2), :],
        send_ref, layers, rows, 4 * layers,
    )


def wells_kernel(recv_ref, wells_ref):
    members, stride = 128, recv_ref.shape[0] // 128
    wells_ref[...] = recv_ref[pl.ds(stride - 1, members, stride=stride), :].T[:STEPS]


def give_kernel(core_ref, recv_ref, after_ref, give_ref):
    members, stride = 128, recv_ref.shape[0] // 128
    for core in range(2):
        @pl.when(core_ref[0] == core)
        def _():
            for j in range(8):
                give_ref[pl.ds(members * j, members), :] = recv_ref[
                    pl.ds(8 * (1 - core) + j, members, stride=stride - core), :
                ]


def steps_kernel(known_ref, own_ref, mix_ref):
    members = own_ref.shape[1]
    y = own_ref[...]
    step_id = lax.broadcasted_iota(jnp.int32, y.shape, 0)
    means = jnp.sum(y, axis=1, keepdims=True) * (1.0 / members)
    spreads = y - means
    gains = jnp.zeros_like(y)
    weights_all = jnp.zeros_like(y)
    for k in range(STEPS):
        spread = spreads[k:k + 1]
        variance = known_ref[STEPS + k:STEPS + k + 1, :]
        products = jnp.sum(spreads * spread, axis=1, keepdims=True)
        denom = products[k:k + 1] / (members - 1) + variance
        alpha = 1.0 / (1.0 + jnp.sqrt(variance / denom))
        shift = known_ref[k:k + 1, :] - means[k:k + 1]
        weights = shift - alpha * spread
        factor = 1.0 / ((members - 1) * denom)
        earlier = jnp.sum(weights_all * spread, axis=1, keepdims=True)
        gain = factor * (spread + jnp.sum(gains * earlier, axis=0, keepdims=True))
        rate = factor * products
        means = means + rate * shift
        spreads = spreads - (rate * alpha) * spread
        gains = jnp.where(step_id == k, gain, gains)
        weights_all = jnp.where(step_id == k, weights, weights_all)
    mix_ref[...] = lax.dot_general(
        weights_all, gains, (((0,), (0,)), ((), ())), precision=HIGHEST,
        preferred_element_type=jnp.float32,
    )


def apply_kernel(core_ref, recv_ref, got_ref, own_mix_ref, other_mix_ref, perm_out, head_out, kept, taken, sems):
    members, stride = 128, recv_ref.shape[0] // 128
    layers = kept.shape[0]
    core = core_ref[0]
    mix = jnp.where(core == 0, own_mix_ref[...], other_mix_ref[...])
    mix_high, mix_low = split_bf16(mix)
    mixes = jnp.concatenate([mix_high, mix_high, mix_low], 1)

    def copies(own_out, got_out, layer):
        return [
            pltpu.make_async_copy(kept.at[layer], own_out.at[layer], sems.at[0, layer]),
            pltpu.make_async_copy(taken.at[layer], got_out.at[layer], sems.at[1, layer]),
        ]

    def run(first, step, own_out, got_out):
        for layer in range(layers):
            x = jnp.concatenate(
                [recv_ref[pl.ds(first + 2 * layer + r, members, stride=step), :] for r in range(2)]
                + [got_ref[pl.ds(members * (2 * layer + r), members), :] for r in range(2)], 1
            )
            high, low = split_bf16(x)
            x = x + jnp.dot(
                mixes, jnp.concatenate([high, low, high], 0), preferred_element_type=jnp.float32
            )
            columns = x.shape[1] // 4
            for place, ref in enumerate((kept, taken)):
                for r in range(2):
                    at = (2 * place + r) * columns
                    ref[layer, pl.ds(r, members, stride=2), :] = x[:, at:at + columns]
            for copy in copies(own_out, got_out, layer):
                copy.start()
        for layer in range(layers):
            for copy in copies(own_out, got_out, layer):
                copy.wait()

    @pl.when(core == 0)
    def _():
        run(0, stride, head_out, perm_out)

    @pl.when(core == 1)
    def _():
        run(8, stride - 1, perm_out, head_out)


def split_bf16(x):
    high = x.astype(jnp.bfloat16)
    return high, (x - high.astype(jnp.float32)).astype(jnp.bfloat16)


def call(kernel, out, in_specs, scratch=()):
    return pl.pallas_call(
        kernel, out_shape=out, in_specs=in_specs,
        out_specs=jax.tree.map(lambda _: VMEM, out),
        scratch_shapes=list(scratch), compiler_params=PARAMS,
    )


def f32(*shape):
    return jax.ShapeDtypeStruct(shape, jnp.float32)


def exchange(send, parts):
    return lax.all_to_all(
        send.reshape(parts, -1, 1, send.shape[1]), "gx", split_axis=0, concat_axis=0, tiled=True
    ).reshape(send.shape)


def heads_part(cells, order, perm, rech, perm_far, rech_far, perm_recv):
    layers, rows, columns = perm.shape
    field = pltpu.VMEM((2, layers, rows, columns), jnp.float32)
    padded = pltpu.VMEM((2, layers, rows + 2 * PAD, columns), jnp.float32)
    send = call(
        heads_kernel, f32(rows // 2 * (4 * layers + 1), columns), [HBM, HBM] + [VMEM] * 4,
        [pltpu.SMEM(cells.shape, jnp.int32), pltpu.SMEM(order.shape, jnp.int32), pltpu.SemaphoreType.DMA((2,))]
        + [padded, padded] + [field] * 8 + [padded, padded],
    )(cells, order, perm, rech, perm_far, rech_far)
    return exchange(send, rows // 2)


def rest_part(cells, order, perm, rech, perm_far, rech_far, perm_recv):
    rows, columns = perm.shape[1:]
    return jnp.concatenate([perm_recv, jnp.zeros((rows // 2, columns), jnp.float32)], 0)


def perm_part(perm, perm_far):
    layers, rows, columns = perm.shape
    send = call(pack_kernel, f32(rows // 2 * 4 * layers, columns), [VMEM, VMEM])(perm, perm_far)
    parts, depth = rows // 2, rows // 2 // PLANE
    along_z = [[z * PLANE + spot for z in range(depth)] for spot in range(PLANE)]
    in_plane = [[z * PLANE + spot for spot in range(PLANE)] for z in range(depth)]

    def stage(x, groups):
        return lax.all_to_all(
            x.reshape(parts, -1, 1, columns), "gx", split_axis=0, concat_axis=0, tiled=True,
            axis_index_groups=groups,
        )

    x = stage(send, along_z).reshape(depth, PLANE, -1, columns).swapaxes(0, 1)
    x = stage(x, in_plane).reshape(PLANE, depth, -1, columns).swapaxes(0, 1)
    return x.reshape(send.shape)


def no_part(perm, perm_far):
    layers, rows, columns = perm.shape
    return jnp.zeros((rows // 2 * 4 * layers, columns), jnp.float32)


def body(log_perm, recharge, well_cells, observed, variances, well_order):
    layers, _, rows, columns = log_perm.shape
    parts = lax.axis_size("gx")
    core = lax.axis_index("gy").astype(jnp.int32).reshape(1)
    swap = [(0, 1), (1, 0)]
    perm = log_perm.reshape(layers, rows, columns)
    perm_far = lax.ppermute(perm, "gy", swap)
    rech_far = lax.ppermute(recharge, "gy", swap)
    perm, recharge, well_cells, well_order, observed, variances = (
        pltpu.with_memory_space_constraint(x, pltpu.HBM)
        for x in (perm, recharge, well_cells, well_order, observed, variances)
    )
    perm, recharge, known = call(
        stage_kernel, (f32(*perm.shape), f32(*recharge.shape), f32(2 * STEPS, parts)), [HBM] * 5,
        [pltpu.SMEM(well_order.shape, jnp.int32), pltpu.SMEM(observed.shape, jnp.float32)]
        + [pltpu.SMEM(variances.shape, jnp.float32), pltpu.SemaphoreType.DMA((2, layers))]
        + [pltpu.SemaphoreType.DMA((3,))],
    )(perm, recharge, well_order, observed, variances)
    perm_recv = lax.cond(core[0] == 1, perm_part, no_part, perm, perm_far)
    recv = lax.cond(
        core[0] == 0, heads_part, rest_part,
        well_cells, well_order, perm, recharge, perm_far, rech_far, perm_recv,
    )
    own = call(wells_kernel, f32(STEPS, parts), [VMEM])(recv)
    give = call(give_kernel, f32(parts * 2 * layers, columns), [SMEM, VMEM, VMEM])(core, recv, own)
    got = lax.ppermute(give, "gy", swap)
    mix = call(
        steps_kernel, f32(parts, parts), [VMEM] * 2
    )(known, own)
    other_mix = lax.ppermute(mix, "gy", swap)
    field = (layers, parts * 2, columns)
    post_perm, post_head = pl.pallas_call(
        apply_kernel, out_shape=(f32(*field), f32(*field)),
        in_specs=[SMEM] + [VMEM] * 4, out_specs=(HBM, HBM),
        scratch_shapes=[pltpu.VMEM(field, jnp.float32)] * 2 + [pltpu.SemaphoreType.DMA((2, layers))],
        compiler_params=PARAMS,
    )(core, recv, got, mix, other_mix)
    shape = (layers, parts, 2, columns)
    return post_perm.reshape(shape), post_head.reshape(shape)


def solution(mesh):
    placed = (P(None, "gx", None, "gy"), P(None, None, "gy"), P(), P(), P(), P())
    return jax.shard_map(
        body,
        mesh=mesh,
        in_specs=placed,
        out_specs=(P(None, None, "gx", "gy"), P(None, None, "gx", "gy")),
        check_vma=False,
    )
```
